32 devices in a mesh: role: 2 (over x), seq: 4 (over z), tp: 4 (over y, core).
Axes of the slice: x: 2, y: 2, z: 4, core: 2. Of those that a mesh axis runs over, the one named last changes fastest.
Arguments:
- hidden: bfloat16 [2048, 8192], P(('role', 'seq')), may hold values from -11 to 11
- w_query: bfloat16 [8192, 4096], P(None, 'tp'), may hold values from -0.0625 to 0.0625
- w_key: bfloat16 [896, 4096], P(None, 'tp'), may hold values from -0.1875 to 0.1875
- w_value: bfloat16 [896, 4096], P(None, 'tp'), may hold values from -0.1875 to 0.1875
- enc_gain: float32 [896], replicated, may hold values from 0.1 to 1.9
- w_in: bfloat16 [896, 1792], replicated, may hold values from -0.1875 to 0.1875
- w_out: bfloat16 [1792, 896], replicated, may hold values from -0.125 to 0.125
- db_states: bfloat16 [128, 128, 896], P(('role', 'seq'), 'tp'), may hold values from -24 to 24
- neighbours: int32 [32, 2], P(('role', 'seq')), may hold values from 0 to 127, as said below
- d_attended: bfloat16 [2048, 4096], P(('role', 'seq'), 'tp'), may hold values from -24 to 24
Outputs:
- attended: bfloat16 [2048, 4096], P(('role', 'seq'), 'tp')
- grad_rows: bfloat16 [128, 128, 896], P(('role', 'seq'), 'tp')
The draws below stay inside these ranges and needn't reach their ends.
Inputs may be any that keep to these rules, and one draw needn't show every extreme that they name: Database rows; shard g of role+seq holds rows g * 16 to (g + 1) * 16 - 1. Of the 8 neighbours of the stretches on one index of role+seq, at most 2 lie in one shard (repeats counted), and exactly 2 in some shard.
All inputs are finite; a program needn't handle non-finite values.
Results may differ from the reference program's by a relative error of at most 0.02.
The reference program's roundings to bfloat16 on the way count: a program that leaves them out, or rounds other values in their place, can miss the bound.
Values may be sent and summed in bfloat16 or wider, within the bound.
No kernel may reach another device: no remote copies, remote signals or barrier semaphores. Data moves between devices by JAX's collectives and lax.ppermute only.
A program may use at most 128 MiB of HBM per device.

```python
import math
import jax
import jax.numpy as jnp
from jax import lax

D = 8192
HEADS = 32
HD = 128
DE = 896
FE = 1792
NT = 128
STRETCH = 64
K_NB = 2
TOK_DEV = 256
R_DEV = 16
GROUPS = 8
TOKENS = 2048
CH_DEV = 4
STRETCHES = 32
DB_ROWS = 128
FEAT = 4096
N_ROLE = 2
N_SEQ = 4


def draw_hidden(key, part):
    key = jax.random.fold_in(key, 5)
    base_key = jax.random.fold_in(key, 0)
    base = jax.random.truncated_normal(base_key, -6.0, 6.0, (TOKENS, D), jnp.float32)
    return base.astype(jnp.bfloat16)


def draw_db_states(key, part):
    key = jax.random.fold_in(key, 7)
    base_key, column_key, token_key = jax.random.split(key, 3)
    columns = jnp.exp(jax.random.uniform(column_key, (1, 1, DE), jnp.float32, math.log(0.3), math.log(3.0)))
    tokens = jnp.exp(jax.random.uniform(token_key, (DB_ROWS, NT, 1), jnp.float32, math.log(0.5), math.log(2.0)))
    base = jax.random.truncated_normal(base_key, -4.0, 4.0, (DB_ROWS, NT, DE), jnp.float32)
    return (base * columns * tokens).astype(jnp.bfloat16)


def draw_neighbours(key, part):
    key = jax.random.fold_in(key, 11)
    hot_key, shuffle_key, order_key, row_key = jax.random.split(key, 4)
    groups = DB_ROWS // R_DEV
    slot_count = CH_DEV * K_NB
    hot_owner = jax.random.randint(hot_key, (), 0, groups)
    shuffles = jax.vmap(lambda sub_key: jax.random.permutation(sub_key, groups - 1))(jax.random.split(shuffle_key, groups))
    unit_of = jnp.maximum(jnp.arange(slot_count) - 2, 0) // 2 % (groups - 1)
    others = shuffles[:, unit_of]
    others = others + (others >= hot_owner).astype(jnp.int32)
    owners = jnp.where(jnp.arange(slot_count)[None, :] < 2, hot_owner, others)
    orders = jax.vmap(lambda sub_key: jax.random.permutation(sub_key, slot_count))(jax.random.split(order_key, groups))
    owners = jnp.take_along_axis(owners, orders, axis=1)
    row_pick = jax.random.randint(row_key, (groups, slot_count), 0, R_DEV)
    return (owners * R_DEV + row_pick).reshape(STRETCHES, K_NB).astype(jnp.int32)


def shard_levels(stream_key, shape, cuts, low, high):
    level, own = 1.0, jax.random.fold_in(stream_key, 6)
    for position, parts in cuts:
        draws = jnp.exp(jax.random.uniform(jax.random.fold_in(own, position), (parts,), jnp.float32, low / len(cuts), high / len(cuts)))
        level = level * jnp.repeat(draws, shape[position] // parts).reshape([-1 if axis == position else 1 for axis in range(len(shape))])
    return level


def scatter_about(own_key, dims, width, reach, pieces=(), kind=jnp.bfloat16):
    values = width * jax.random.normal(own_key, dims, jnp.float32)
    if pieces:
        values = values * shard_levels(own_key, dims, pieces, -0.22, 0.18)
    return jnp.clip(values, -reach, reach).astype(kind)


def setup_inputs(seed: int = 0) -> dict:
    arg_keys = jax.random.split(jax.random.key(seed), 11)
    return {
        "hidden": draw_hidden(jax.random.fold_in(arg_keys[10], 71), 0),
        "w_query": scatter_about(arg_keys[1], (D, FEAT), D ** -0.5, 0.0625, ((1, 4),)),
        "w_key": scatter_about(arg_keys[2], (DE, FEAT), DE ** -0.5, 0.1875, ((1, 4),)),
        "w_value": scatter_about(arg_keys[3], (DE, FEAT), DE ** -0.5, 0.1875, ((1, 4),)),
        "enc_gain": jnp.clip(1.0 + 0.18 * jax.random.normal(arg_keys[4], (DE,), jnp.float32), 0.1, 1.9),
        "w_in": scatter_about(arg_keys[5], (DE, FE), DE ** -0.5, 0.1875),
        "w_out": scatter_about(arg_keys[6], (FE, DE), FE ** -0.5, 0.125),
        "db_states": draw_db_states(jax.random.fold_in(arg_keys[10], 71), 0),
        "neighbours": draw_neighbours(jax.random.fold_in(arg_keys[10], 71), 0),
        "d_attended": scatter_about(arg_keys[9], (TOKENS, FEAT), 4.0, 24.0, ((0, 8), (1, 4))),
    }


EPS = 1e-06

def encode(flat_rows, enc_gain, w_in, w_out):
    row_values = flat_rows.astype(jnp.float32)
    inverse = lax.rsqrt(lax.optimization_barrier(jnp.mean(row_values * row_values, axis=-1, keepdims=True)) + EPS)
    normed = (row_values * inverse * enc_gain).astype(jnp.bfloat16)
    pre_act = jnp.dot(normed, w_in, preferred_element_type=jnp.float32)
    active = jax.nn.gelu(pre_act).astype(jnp.bfloat16)
    encoded = (row_values + jnp.dot(active, w_out, preferred_element_type=jnp.float32)).astype(jnp.bfloat16)
    return (encoded, inverse, pre_act)

def encode_back(flat_rows, inverse, pre_act, row_grad, enc_gain, w_in, w_out):
    row_values = flat_rows.astype(jnp.float32)
    upstream = row_grad.astype(jnp.bfloat16)
    d_act = jnp.dot(upstream, w_out.T, preferred_element_type=jnp.float32)
    d_pre = jax.vjp(jax.nn.gelu, pre_act)[1](d_act)[0]
    d_norm = jnp.dot(d_pre.astype(jnp.bfloat16), w_in.T, preferred_element_type=jnp.float32)
    scaled = d_norm * enc_gain
    cubed = inverse * inverse * inverse
    back_term = inverse * scaled - row_values * cubed * lax.optimization_barrier(jnp.mean(scaled * row_values, axis=-1, keepdims=True))
    return (row_grad + back_term).astype(jnp.bfloat16)

def attend(queries, key_rows, value_rows, score_scale):
    scores = jnp.einsum('bqhe,bkhe->bhqk', queries.astype(jnp.float32), key_rows.astype(jnp.float32)) * score_scale
    maximum = lax.optimization_barrier(jnp.max(scores, axis=-1, keepdims=True))
    weights = jnp.exp(scores - maximum)
    probability = weights / lax.optimization_barrier(jnp.sum(weights, axis=-1, keepdims=True))
    rounded = probability.astype(jnp.bfloat16)
    outputs = jnp.einsum('bhqk,bkhe->bqhe', rounded.astype(jnp.float32), value_rows.astype(jnp.float32))
    return (outputs, probability, rounded)

def attend_back(queries, value_rows, probability, rounded, cotangent, score_scale):
    value_grads = jnp.einsum('bhqk,bqhe->bkhe', rounded.astype(jnp.float32), cotangent.astype(jnp.float32))
    dprobs = jnp.einsum('bqhe,bkhe->bhqk', cotangent.astype(jnp.float32), value_rows.astype(jnp.float32))
    centre = lax.optimization_barrier(jnp.sum(probability * dprobs, axis=-1, keepdims=True))
    dscores = (probability * (dprobs - centre)).astype(jnp.bfloat16)
    key_grads = jnp.einsum('bhqk,bqhe->bkhe', dscores.astype(jnp.float32), queries.astype(jnp.float32)) * score_scale
    return (key_grads, value_grads)

def reference(hidden, w_query, w_key, w_value, enc_gain, w_in, w_out, db_states, neighbours, d_attended):
    score_scale = HD ** (-0.5)
    seq_len = TOK_DEV * N_SEQ
    stretch_seq = seq_len // STRETCH
    span = K_NB * NT
    flat_ids = neighbours.reshape(-1).astype(jnp.int32)
    cited = jnp.take(db_states, flat_ids, axis=0).reshape(-1, DE)
    encoded, inverse, pre_act = encode(cited, enc_gain, w_in, w_out)
    key_rows = jnp.dot(encoded, w_key, preferred_element_type=jnp.float32).astype(jnp.bfloat16)
    value_rows = jnp.dot(encoded, w_value, preferred_element_type=jnp.float32).astype(jnp.bfloat16)
    zero_stretch = ((0, 0), (1, 0), (0, 0), (0, 0), (0, 0))
    key_rows = jnp.pad(key_rows.reshape(N_ROLE, stretch_seq, span, HEADS, HD), zero_stretch)
    key_rows = key_rows.reshape(N_ROLE * (stretch_seq + 1), span, HEADS, HD)
    value_rows = jnp.pad(value_rows.reshape(N_ROLE, stretch_seq, span, HEADS, HD), zero_stretch)
    value_rows = value_rows.reshape(N_ROLE * (stretch_seq + 1), span, HEADS, HD)
    queries = jnp.dot(hidden, w_query, preferred_element_type=jnp.float32).astype(jnp.bfloat16)
    edges = ((0, 0), (1, STRETCH - 1), (0, 0), (0, 0))
    block_q = jnp.pad(queries.reshape(N_ROLE, seq_len, HEADS, HD), edges)
    block_q = block_q.reshape(N_ROLE * (stretch_seq + 1), STRETCH, HEADS, HD)
    outputs, probability, rounded = attend(block_q, key_rows, value_rows, score_scale)
    outputs = outputs.reshape(N_ROLE, (stretch_seq + 1) * STRETCH, HEADS * HD)[:, 1:seq_len + 1]
    attended = outputs.reshape(TOKENS, HEADS * HD).astype(jnp.bfloat16)
    block_d = jnp.pad(d_attended.reshape(N_ROLE, seq_len, HEADS, HD), edges)
    block_d = block_d.reshape(N_ROLE * (stretch_seq + 1), STRETCH, HEADS, HD)
    key_grads, value_grads = attend_back(block_q, value_rows, probability, rounded, block_d, score_scale)
    key_back = key_grads.reshape(N_ROLE, stretch_seq + 1, span, HEADS * HD)[:, 1:]
    key_back = key_back.reshape(-1, HEADS * HD).astype(jnp.bfloat16)
    value_back = value_grads.reshape(N_ROLE, stretch_seq + 1, span, HEADS * HD)[:, 1:]
    value_back = value_back.reshape(-1, HEADS * HD).astype(jnp.bfloat16)
    slot_grad = jnp.dot(key_back, w_key.T, preferred_element_type=jnp.float32)
    slot_grad = slot_grad + jnp.dot(value_back, w_value.T, preferred_element_type=jnp.float32)
    row_grad = jax.ops.segment_sum(slot_grad.reshape(STRETCHES * K_NB, NT * DE), flat_ids, num_segments=DB_ROWS)

    def backward_group(pair):
        rows_block, grad_block = pair
        unused, inverse_block, pre_block = encode(rows_block, enc_gain, w_in, w_out)
        return encode_back(rows_block, inverse_block, pre_block, grad_block, enc_gain, w_in, w_out)
    grads = lax.map(backward_group, (db_states.reshape(GROUPS, R_DEV * NT, DE), row_grad.reshape(GROUPS, R_DEV * NT, DE)))
    return (attended, grads.reshape(DB_ROWS, NT, DE))
```

```python
import functools

import jax
import jax.numpy as jnp
from jax import lax
from jax.experimental import pallas as pl
from jax.experimental.pallas import tpu as pltpu
from jax.sharding import PartitionSpec as P

HD = 128
STRETCH = 64
EPS = 1e-06
GELU_A = 0.7978845608028654
GELU_B = 0.044715
F32 = jnp.float32
BF16 = jnp.bfloat16


def params(mib):
    return pltpu.CompilerParams(vmem_limit_bytes=mib * 1024 * 1024)


def dot(a, b):
    return jnp.dot(a, b, preferred_element_type=F32)


def dot_nt(a, b):
    return lax.dot_general(a, b, (((1,), (1,)), ((), ())), preferred_element_type=F32)


def dot_tn(a, b):
    return lax.dot_general(a, b, (((0,), (0,)), ((), ())), preferred_element_type=F32)


def whole(shape):
    return pl.BlockSpec(shape, lambda *_: (0,) * len(shape))


def smem():
    return pl.BlockSpec(memory_space=pltpu.SMEM)


def vmem():
    return pl.BlockSpec(memory_space=pltpu.VMEM)


def anywhere():
    return pl.BlockSpec(memory_space=pl.ANY)


def hbm(*arrays):
    return [pltpu.with_memory_space_constraint(array, pltpu.HBM) for array in arrays]


def tiles(size, part):
    return [(at, min(part, size - at)) for at in range(0, size, part)]


def exchange_masks(groups, peers):
    masks = range(1, groups)
    far = sorted([m for m in masks if m & (peers // 2)], reverse=True)
    near = sorted([m for m in masks if not m & (peers // 2)], key=lambda m: (m % peers != 0, -m))
    return [0] + near[:2] + far + near[2:]


def each_request(ids_ref, g, first, row_count, capacity, act):
    fan_out = ids_ref.shape[1]
    rank = jnp.int32(0)
    for s in range(ids_ref.shape[2] * fan_out):
        local = ids_ref[g, s % fan_out, s // fan_out] - first
        mine = (local >= 0) & (local < row_count)
        place = jnp.minimum(rank, capacity - 1)

        @pl.when(mine)
        def _():
            act(jnp.clip(local, 0, row_count - 1), place)

        rank = rank + mine.astype(jnp.int32)


def norm_of(x, gain):
    inverse = lax.rsqrt(jnp.mean(x * x, axis=-1, keepdims=True) + EPS)
    return (x * inverse * gain).astype(BF16), inverse


def encode_kernel(
    gain_hbm, x_hbm, w_in_hbm, w_out_hbm, enc_ref,
    gain_ref, x_ref, w_in, w_out, normed, active, sems, in_sems,
):
    rows, width = x_ref.shape
    hidden = w_in.shape[1]
    x_copy = pltpu.make_async_copy(x_hbm, x_ref, sems.at[0])
    x_copy.start()
    gain_copy = pltpu.make_async_copy(gain_hbm, gain_ref, sems.at[2])
    gain_copy.start()
    parts = [pl.ds(at, part) for at, part in tiles(hidden, hidden // 2)]
    in_copies = []
    for i, cols in enumerate(parts):
        copy = pltpu.make_async_copy(w_in_hbm.at[:, cols], w_in.at[:, cols], in_sems.at[i])
        copy.start()
        in_copies.append(copy)
    out_copy = pltpu.make_async_copy(w_out_hbm, w_out, sems.at[1])
    x_copy.wait()
    gain_copy.wait()
    normed[...], _ = norm_of(x_ref[...].astype(F32), gain_ref[...].reshape(1, width))
    for i, cols in enumerate(parts):
        in_copies[i].wait()
        if i == 0:
            out_copy.start()
        for at, part in tiles(cols.size, 256):
            band = pl.ds(cols.start + at, part)
            pre = dot(normed[...], w_in[:, band])
            tanh = jnp.tanh(GELU_A * (pre + GELU_B * (pre * pre * pre)))
            active[:, band] = (pre * (0.5 * (1.0 + tanh))).astype(BF16)
    out_copy.wait()
    for at, part in tiles(rows, 256):
        band = pl.ds(at, part)
        total = x_ref[band, :].astype(F32) + dot(active[band, :], w_out[...])
        enc_ref[band, :] = total.astype(BF16)


def encode(flat_rows, enc_gain, w_in, w_out):
    rows, width = flat_rows.shape
    hidden = w_in.shape[1]
    return pl.pallas_call(
        encode_kernel,
        in_specs=[anywhere()] * 4,
        out_specs=vmem(),
        out_shape=pltpu.VMEM((rows, width), BF16),
        scratch_shapes=[
            pltpu.VMEM((width,), F32),
            pltpu.VMEM((rows, width), BF16),
            pltpu.VMEM((width, hidden), BF16),
            pltpu.VMEM((hidden, width), BF16),
            pltpu.VMEM((rows, width), BF16),
            pltpu.VMEM((rows, hidden), BF16),
            pltpu.SemaphoreType.DMA((3,)),
            pltpu.SemaphoreType.DMA((2,)),
        ],
        compiler_params=params(14),
        cost_estimate=pl.CostEstimate(
            flops=4 * rows * width * hidden,
            bytes_accessed=4 * width * hidden + 4 * rows * width,
            transcendentals=rows * hidden,
        ),
        name="encode",
    )(*hbm(enc_gain, flat_rows, w_in, w_out))


def send_kernel(masks, ids_ref, me_ref, enc_ref, h_hbm, *refs):
    out_refs, (h_ref, h_sem, sems) = refs[:-3], refs[-3:]
    h_copy = pltpu.make_async_copy(h_hbm, h_ref, h_sem)
    h_copy.start()
    row_count = enc_ref.shape[0]
    capacity = out_refs[0].shape[0]
    me = me_ref[0]

    def copy_of(k, row, place):
        return pltpu.make_async_copy(enc_ref.at[row], out_refs[k].at[place], sems.at[k, place])

    for k, mask in enumerate(masks):
        each_request(
            ids_ref, me ^ mask, me * row_count, row_count, capacity,
            lambda row, place: copy_of(k, row, place).start(),
        )
    for k, mask in enumerate(masks):
        each_request(
            ids_ref, me ^ mask, me * row_count, row_count, capacity,
            lambda row, place: copy_of(k, row, place).wait(),
        )
    h_copy.wait()


def send_rows(all_ids, me, encoded, tokens, capacity, masks):
    row_count, piece, width = encoded.shape
    groups = all_ids.shape[0]
    return pl.pallas_call(
        functools.partial(send_kernel, masks),
        in_specs=[smem(), smem(), vmem(), anywhere()],
        out_specs=[anywhere()] * groups + [vmem()],
        out_shape=[jax.ShapeDtypeStruct((capacity, piece, width), BF16)] * groups
        + [pltpu.VMEM(tokens.shape, BF16)],
        scratch_shapes=[
            pltpu.SemaphoreType.DMA,
            pltpu.SemaphoreType.DMA((groups, capacity)),
        ],
        compiler_params=params(4),
        name="send_rows",
    )(all_ids, me, encoded, *hbm(tokens))


def query_kernel(h_ref, d_ref, w_hbm, out_ref, edge_ref, blocks, total, sems):
    part = blocks.shape[1]
    count = h_ref.shape[1] // part
    copies = [
        pltpu.make_async_copy(w_hbm.at[pl.ds(i * part, part), :], blocks.at[i % 3], sems.at[i % 3])
        for i in range(count)
    ]
    for copy in copies[:3]:
        copy.start()
    for i in range(count):
        copies[i].wait()
        value = dot(h_ref[:, pl.ds(i * part, part)], blocks[i % 3])
        total[...] = value if i == 0 else total[...] + value
        if i + 3 < count:
            copies[i + 3].start()
    out_ref[...] = total[...].astype(BF16)
    edge_ref[:STRETCH, :] = total[:STRETCH, :].astype(BF16)
    edge_ref[STRETCH:, :] = d_ref[:STRETCH, :]


def query(tokens, w_query, cotangent):
    count, depth = tokens.shape
    feats = w_query.shape[1]
    return pl.pallas_call(
        query_kernel,
        in_specs=[vmem()] * 2 + [anywhere()],
        out_specs=[vmem()] * 2,
        out_shape=[
            jax.ShapeDtypeStruct((count, feats), BF16),
            jax.ShapeDtypeStruct((2 * STRETCH, feats), BF16),
        ],
        scratch_shapes=[
            pltpu.VMEM((3, 1024, feats), BF16),
            pltpu.VMEM((count, feats), F32),
            pltpu.SemaphoreType.DMA((3,)),
        ],
        compiler_params=params(12),
        cost_estimate=pl.CostEstimate(
            flops=2 * count * depth * feats,
            bytes_accessed=2 * depth * feats + 4 * count * feats,
            transcendentals=0,
        ),
        name="query",
    )(tokens, cotangent, *hbm(w_query))


def places_of(ids_ref, me, row_count, capacity):
    fan_out, stretch_count = ids_ref.shape
    ids = [ids_ref[s % fan_out, s // fan_out] for s in range(fan_out * stretch_count)]
    if row_count & (row_count - 1):
        owners = [lax.div(row, jnp.int32(row_count)) for row in ids]
    else:
        bits = jnp.int32(row_count.bit_length() - 1)
        owners = [lax.shift_right_logical(row, bits) for row in ids]
    places = []
    for s, owner in enumerate(owners):
        rank = jnp.int32(0)
        for other in owners[:s]:
            rank = rank + (other == owner).astype(jnp.int32)
        places.append((owner ^ me, jnp.minimum(rank, capacity - 1)))
    return places


def pick_kernel(row_count, masks, halves, ids_ref, me_ref, *refs):
    arrived_refs, refs = refs[: len(masks)], refs[len(masks) :]
    out_refs, sems = refs[:halves], refs[halves]
    capacity = arrived_refs[0].shape[0]
    slots = out_refs[0].shape[0]
    for s, (mask, rank) in enumerate(places_of(ids_ref, me_ref[0], row_count, capacity)):
        out_ref = out_refs[s // slots]
        for here, ref in zip(masks, arrived_refs):

            @pl.when(mask == here)
            def _():
                pltpu.make_async_copy(ref.at[rank], out_ref.at[s % slots], sems.at[s]).start()

    for s in range(slots * halves):
        out_ref = out_refs[s // slots].at[s % slots]
        pltpu.make_async_copy(arrived_refs[0].at[0], out_ref, sems.at[s]).wait()


def pick_rows(neighbours, me, arrived, row_count, masks, halves):
    capacity, piece, width = arrived[0].shape
    slots = neighbours.size
    return pl.pallas_call(
        functools.partial(pick_kernel, row_count, masks, halves),
        in_specs=[smem(), smem()] + [anywhere()] * len(arrived),
        out_specs=[anywhere()] * halves,
        out_shape=[jax.ShapeDtypeStruct((slots // halves, piece, width), BF16)] * halves,
        scratch_shapes=[pltpu.SemaphoreType.DMA((slots,))],
        compiler_params=params(4),
        name="pick_rows",
    )(neighbours, me, *arrived)


def return_kernel(row_count, masks, counts, ids_ref, me_ref, *refs):
    share_refs, refs = refs[: sum(counts)], refs[sum(counts) :]
    out_refs, (total, sems) = refs[: len(masks)], refs[len(masks) :]
    shares = []
    for count in counts:
        shares.append(share_refs[:count])
        share_refs = share_refs[count:]
    capacity = out_refs[0].shape[0]
    slots = total.shape[0]
    for s, (mask, rank) in enumerate(places_of(ids_ref, me_ref[0], row_count, capacity)):
        value = None
        for share in shares:
            each = slots // len(share)
            part = share[s // each][s % each].astype(F32)
            value = part if value is None else value + part
        total[s] = value.astype(BF16)
        for here, ref in zip(masks, out_refs):

            @pl.when(mask == here)
            def _():
                pltpu.make_async_copy(total.at[s], ref.at[rank], sems.at[s]).start()

    for s in range(slots):
        pltpu.make_async_copy(total.at[s], out_refs[0].at[0], sems.at[s]).wait()


def return_grads(neighbours, me, shares, row_count, masks, capacity):
    _, piece, width = shares[0][0].shape
    slots = neighbours.size
    groups = len(masks)
    counts = [len(share) for share in shares]
    return pl.pallas_call(
        functools.partial(return_kernel, row_count, masks, counts),
        in_specs=[smem(), smem()] + [vmem()] * sum(counts),
        out_specs=[anywhere()] * groups,
        out_shape=[jax.ShapeDtypeStruct((capacity, piece, width), BF16)] * groups,
        scratch_shapes=[
            pltpu.VMEM((slots, piece, width), BF16),
            pltpu.SemaphoreType.DMA((slots,)),
        ],
        compiler_params=params(8),
        name="return_grads",
    )(neighbours, me, *[part for share in shares for part in share])


def fill_keys(x, wk_ref, wv_ref, keys, values):
    for w_ref, out in ((wk_ref, keys), (wv_ref, values)):
        for at, part in tiles(w_ref.shape[1], 256):
            cols = pl.ds(at, part)
            out[:, cols] = dot(x, w_ref[:, cols]).astype(BF16)


def project_kernel(count, *refs):
    piece_refs, (wk_ref, wv_ref, *out_refs) = refs[:-2 - 2 * count], refs[-2 - 2 * count :]
    each = len(piece_refs) // count
    for i in range(count):
        x = [ref[...] for ref in piece_refs[i * each : (i + 1) * each]]
        x = jnp.concatenate(x, axis=0)
        fill_keys(x, wk_ref, wv_ref, out_refs[2 * i], out_refs[2 * i + 1])


def project(halves, w_key, w_value):
    pieces = [piece for half in halves for piece in half]
    rows, width = pieces[0].shape
    rows *= len(halves[0])
    feats = w_key.shape[1]
    count = len(halves)
    out = pl.pallas_call(
        functools.partial(project_kernel, count),
        in_specs=[vmem()] * (len(pieces) + 2),
        out_specs=[vmem()] * (2 * count),
        out_shape=[jax.ShapeDtypeStruct((rows, feats), BF16)] * (2 * count),
        compiler_params=params(16),
        cost_estimate=pl.CostEstimate(
            flops=4 * count * rows * width * feats,
            bytes_accessed=4 * width * feats + 2 * count * rows * (width + 2 * feats),
            transcendentals=0,
        ),
        name="project",
    )(*pieces, w_key, w_value)
    return [out[2 * i : 2 * i + 2] for i in range(count)]


def two_blocks(value):
    zeros = jnp.zeros((value.shape[0], HD), value.dtype)
    top = jnp.concatenate([value[:, :HD], zeros], axis=1)
    low = jnp.concatenate([zeros, value[:, HD:]], axis=1)
    return jnp.concatenate([top, low], axis=0)


def moved_up(rows, by):
    return pltpu.roll(rows.astype(F32), rows.shape[0] - by, 0)


def attend_kernel(far_count, first, count, has_edges, *refs):
    near_refs, far_refs, refs = refs[:2], refs[2 : 2 + far_count], refs[2 + far_count :]
    weight_refs, token_refs, refs = refs[:2], refs[2 : 4 + has_edges], refs[4 + has_edges :]
    att_ref, near_dk, near_dv, far_dk, far_dv, far_k, far_v, block_q, block_d = refs
    x = jnp.concatenate([ref[...] for ref in far_refs], axis=0)
    fill_keys(x, *weight_refs, far_k, far_v)
    rows = far_refs[0].shape[0]
    part = rows // count
    block = STRETCH
    for i, out in enumerate((block_q, block_d)):
        own = token_refs[i]
        begin = first * block + block - 16
        size = own.shape[0] - begin if has_edges else count * block + 16
        for at, wide in tiles(own.shape[1], 256):
            cols = pl.ds(at, wide)
            values = own[pl.ds(begin, size), cols]
            if has_edges:
                edge = token_refs[2][pl.ds(i * block, block), cols]
                values = jnp.concatenate([values, edge], axis=0)
            out[:, cols] = moved_up(values, 15)[: count * block].astype(BF16)
    scale = HD ** (-0.5)

    def bands(near, far, c):
        at = [(ref, i) for ref in (near, far) for i in range(far_count)]
        return [(ref, pl.ds(pl.multiple_of(i * rows + c * part, part), part)) for ref, i in at]

    def stretch(c, carry):
        mine = pl.ds(pl.multiple_of(c * block, block), block)
        for h in range(0, block_q.shape[1], 2 * HD):
            cols = pl.ds(h, 2 * HD)
            here = [bands(near_refs[0], far_k, c), bands(near_refs[1], far_v, c)]
            k, v = (jnp.concatenate([ref[b, cols] for ref, b in pair], axis=0) for pair in here)
            q, d = two_blocks(block_q[mine, cols]), two_blocks(block_d[mine, cols])
            scores = dot_nt(k, q) * scale
            weights = jnp.exp(scores - jnp.max(scores, axis=0, keepdims=True))
            probability = weights * (1.0 / jnp.sum(weights, axis=0, keepdims=True))
            rounded = probability.astype(BF16)
            out = dot_tn(rounded, v)
            att_ref[mine, cols] = jnp.concatenate(
                [out[:block, :HD], out[block:, HD:]], axis=1
            ).astype(BF16)
            value_grads = dot(rounded, d).astype(BF16)
            dprobs = dot_nt(v, d)
            centre = jnp.sum(probability * dprobs, axis=0, keepdims=True)
            dscores = (probability * (dprobs - centre)).astype(BF16)
            key_grads = (dot(dscores, q) * scale).astype(BF16)
            for i, (ref, b) in enumerate(bands(near_dk, far_dk, c)):
                ref[b, cols] = key_grads[i * part : (i + 1) * part]
            for i, (ref, b) in enumerate(bands(near_dv, far_dv, c)):
                ref[b, cols] = value_grads[i * part : (i + 1) * part]
        return carry

    lax.fori_loop(0, count, stretch, 0)


def attend(near, far, w_key, w_value, tokens, first, count):
    width, feats = w_key.shape
    rows = near[0].shape[0]
    return pl.pallas_call(
        functools.partial(attend_kernel, len(far), first, count, len(tokens) - 2),
        in_specs=[vmem()] * (4 + len(far) + len(tokens)),
        out_specs=[vmem()] * 5,
        out_shape=[jax.ShapeDtypeStruct((count * STRETCH, feats), BF16)]
        + [jax.ShapeDtypeStruct((rows, feats), BF16)] * 4,
        scratch_shapes=[pltpu.VMEM((rows, feats), BF16)] * 2
        + [pltpu.VMEM((count * STRETCH, feats), BF16)] * 2,
        compiler_params=params(20),
        cost_estimate=pl.CostEstimate(
            flops=4 * rows * width * feats + 40 * rows * STRETCH * feats,
            bytes_accessed=4 * width * feats + 12 * rows * feats,
            transcendentals=2 * rows * STRETCH * feats // HD,
        ),
        name="attend",
    )(*near, *far, w_key, w_value, *tokens)


def terms_kernel(number, *refs):
    *grad_refs, wk_ref, wv_ref, term_ref = refs

    def rows_of(halves):
        part = term_ref.shape[0] // len(halves)
        return jnp.concatenate([ref[pl.ds(number * part, part), :] for ref in halves], axis=0)

    half = len(grad_refs) // 2
    term = dot_nt(rows_of(grad_refs[:half]), wk_ref[...])
    term = term + dot_nt(rows_of(grad_refs[half:]), wv_ref[...])
    term_ref[...] = term.astype(BF16)


def slot_terms(key_grads, value_grads, w_key, w_value, number, rows):
    width, feats = w_key.shape
    return pl.pallas_call(
        functools.partial(terms_kernel, number),
        in_specs=[vmem()] * (len(key_grads) + len(value_grads) + 2),
        out_specs=vmem(),
        out_shape=jax.ShapeDtypeStruct((rows, width), BF16),
        compiler_params=params(16),
        cost_estimate=pl.CostEstimate(
            flops=4 * rows * width * feats,
            bytes_accessed=4 * width * feats + 2 * rows * (width + 2 * feats),
            transcendentals=0,
        ),
        name="slot_terms",
    )(*key_grads, *value_grads, w_key, w_value)


def stage_kernel(
    gain_ref, x_ref, w_in_ref, w_out_ref, inv_ref, slope_ref, w_in_turned, w_out_turned, normed
):
    rows, width = x_ref.shape
    normed[...], inv_ref[...] = norm_of(
        x_ref[...].astype(F32), gain_ref[...].reshape(1, width)
    )
    for at, part in tiles(w_in_ref.shape[1], 256):
        cols = pl.ds(at, part)
        pre = dot(normed[...], w_in_ref[:, cols])
        square = pre * pre
        tanh = jnp.tanh(GELU_A * pre * (1.0 + GELU_B * square))
        slope_ref[:, cols] = 0.5 * (1.0 + tanh) + 0.5 * pre * (1.0 - tanh * tanh) * (
            GELU_A * (1.0 + 3.0 * GELU_B * square)
        )
        w_in_turned[cols, :] = w_in_ref[:, cols].T
        w_out_turned[:, cols] = w_out_ref[cols, :].T


def stage(flat_rows, enc_gain, w_in, w_out):
    rows, width = flat_rows.shape
    hidden = w_in.shape[1]
    return pl.pallas_call(
        stage_kernel,
        in_specs=[vmem()] * 4,
        out_specs=[vmem()] * 4,
        out_shape=[
            jax.ShapeDtypeStruct((rows, 1), F32),
            jax.ShapeDtypeStruct((rows, hidden), F32),
            jax.ShapeDtypeStruct((hidden, width), BF16),
            jax.ShapeDtypeStruct((width, hidden), BF16),
        ],
        scratch_shapes=[pltpu.VMEM((rows, width), BF16)],
        compiler_params=params(24),
        cost_estimate=pl.CostEstimate(
            flops=2 * rows * width * hidden,
            bytes_accessed=8 * width * hidden + 4 * rows * hidden + 4 * rows * width,
            transcendentals=rows * hidden,
        ),
        name="stage",
    )(enc_gain, flat_rows, w_in, w_out)


def encode_back_kernel(
    masks, ids_ref, me_ref, gain_ref, x_ref, inv_ref, slope_ref, w_in_turned, w_out_turned, *refs
):
    arrived_refs, (out_ref, row_grad, upstream, d_pre) = refs[:-4], refs[-4:]
    capacity, piece, width = arrived_refs[0].shape
    row_count = row_grad.shape[0]
    rows = x_ref.shape[0]
    row_grad[...] = jnp.zeros_like(row_grad)
    me = me_ref[0]
    for mask, ref in zip(masks, arrived_refs):

        def add(row, place):
            row_grad[row] += ref[place].astype(F32)

        each_request(ids_ref, me ^ mask, me * row_count, row_count, capacity, add)
    upstream[...] = row_grad[...].reshape(upstream.shape).astype(BF16)
    for at, part in tiles(w_out_turned.shape[1], 256):
        cols = pl.ds(at, part)
        d_act = dot(upstream[...], w_out_turned[:, cols])
        d_pre[:, cols] = (d_act * slope_ref[:, cols]).astype(BF16)
    gain = gain_ref[...].reshape(1, width)
    for at, part in tiles(rows, 256):
        band = pl.ds(at, part)
        scaled = dot(d_pre[band, :], w_in_turned[...]) * gain
        x = x_ref[band, :].astype(F32)
        inverse = inv_ref[band, :]
        mean = jnp.mean(scaled * x, axis=-1, keepdims=True)
        back = inverse * scaled - x * (inverse * inverse * inverse * mean)
        summed = row_grad[at // piece : (at + part) // piece].reshape(part, width)
        out_ref[band, :] = (summed + back).astype(BF16)


def encode_back(all_ids, me, enc_gain, flat_rows, staged, arrived, masks):
    rows, hidden = staged[1].shape
    _, piece, width = arrived[0].shape
    return pl.pallas_call(
        functools.partial(encode_back_kernel, masks),
        in_specs=[smem(), smem()] + [vmem()] * (6 + len(arrived)),
        out_specs=vmem(),
        out_shape=jax.ShapeDtypeStruct((rows, width), BF16),
        scratch_shapes=[
            pltpu.VMEM((rows // piece, piece, width), F32),
            pltpu.VMEM((rows, width), BF16),
            pltpu.VMEM((rows, hidden), BF16),
        ],
        compiler_params=params(28),
        cost_estimate=pl.CostEstimate(
            flops=4 * rows * width * hidden,
            bytes_accessed=4 * width * hidden + 4 * rows * hidden + 8 * rows * width,
            transcendentals=0,
        ),
        name="encode_back",
    )(all_ids, me, enc_gain, flat_rows, *staged, *arrived)


def shift(value, axis, by):
    peers = lax.axis_size(axis)
    pairs = [(i, i + by) for i in range(peers) if 0 <= i + by < peers]
    return lax.ppermute(value, axis, pairs)


def swap(value, axis, bit):
    return lax.ppermute(value, axis, [(i, i ^ bit) for i in range(lax.axis_size(axis))])


def exchange(buffers, masks, later):
    axes = ("role", "seq")
    count = len(buffers)
    arrived = [buffers[0]] + [swap(buffers[k], axes, masks[k]) for k in range(1, count - 2)]
    for early, k in ((1, count - 2), (2, count - 1)):
        arrived[early], value, later = lax.optimization_barrier((arrived[early], buffers[k], later))
        arrived.append(swap(value, axes, masks[k]))
    return arrived, later


def add_up(shares):
    if len(shares) == 1:
        return shares[0]
    return functools.reduce(jnp.add, [share.astype(F32) for share in shares]).astype(BF16)


def body(hidden, w_query, w_key, w_value, enc_gain, w_in, w_out, db_states, neighbours, d_attended):
    groups = lax.axis_size(("role", "seq"))
    shards = lax.axis_size("tp")
    me = lax.axis_index(("role", "seq")).astype(jnp.int32).reshape(1)
    masks = exchange_masks(groups, lax.axis_size("seq"))
    row_count, piece, width = db_states.shape
    stretch_count, fan_out = neighbours.shape
    slots = stretch_count * fan_out
    tokens = hidden.shape[0]
    edge = STRETCH - 1
    capacity = max(2, 2 * ((stretch_count - 1 + groups - 2) // (groups - 1)))
    neighbours = neighbours.T
    all_ids = lax.all_to_all(
        jnp.broadcast_to(neighbours[None], (groups, fan_out, stretch_count)),
        ("role", "seq"), 0, 0, tiled=True,
    )
    flat_rows = db_states.reshape(row_count * piece, width)
    encoded = encode(flat_rows, enc_gain, w_in, w_out)
    *outgoing, hidden = send_rows(
        all_ids, me, encoded.reshape(row_count, piece, width), hidden, capacity, masks
    )
    arrived, (d_attended,) = exchange(outgoing, masks, (d_attended,))
    queries, edges = query(hidden, w_query, d_attended)
    queries, neighbours = lax.optimization_barrier((queries, neighbours))
    count = stretch_count // 2
    first_own, last_own = [
        value.reshape(slots * piece // 2, width)
        for value in pick_rows(neighbours, me, arrived, row_count, masks, 2)
    ]
    first_own, edges = lax.optimization_barrier((first_own, edges))
    edges = shift(edges, "seq", -1)
    bits = [1 << i for i in range(shards.bit_length() - 1)]
    half = shards // 2

    def gathered(pieces):
        for bit in reversed(bits[:-1]):
            pieces.update({mask | bit: swap(pieces[mask], "tp", bit) for mask in list(pieces)})
        return [pieces[mask] for mask in sorted(pieces)]

    first_far = swap(first_own, "tp", half)
    first_near = gathered({0: first_own})
    last_far = swap(last_own, "tp", half)
    last_near = gathered({0: last_own})
    first_kv, last_kv = project([first_near, last_near], w_key, w_value)
    first_far, first_kv, last_kv = lax.optimization_barrier((first_far, first_kv, last_kv))
    first_o, *first_grads = attend(
        first_kv, gathered({half: first_far}), w_key, w_value, (queries, d_attended), 0, count
    )
    first_o, last_far = lax.optimization_barrier((first_o, last_far))
    last_far = gathered({half: last_far})

    rows = slots * piece // 2

    def fold(shares):
        for bit in bits[:-1]:
            for mask in sorted([mask for mask in shares if mask & bit], reverse=True):
                shares[mask ^ bit].append(swap(add_up(shares.pop(mask)), "tp", bit))
        return shares[0]

    def to_send(grads, tied):
        terms = {
            j: [slot_terms(grads[2:3], grads[3:], w_key, w_value, j, rows)]
            for j in reversed(range(1, half))
        }
        near = {0: []}
        near.update({
            j: [slot_terms(grads[0:1], grads[1:2], w_key, w_value, j, rows)]
            for j in reversed(range(1, half))
        })
        tied, grads = lax.optimization_barrier((tied, grads))
        terms[0] = [slot_terms(grads[2:3], grads[3:], w_key, w_value, 0, rows)]
        return add_up(fold(terms)), fold(near), tied

    sent, first_core, edges = to_send(first_grads, edges)
    sent, edges = lax.optimization_barrier((sent, edges))
    first_back = swap(sent, "tp", half)
    last_o, *last_grads = attend(
        last_kv, last_far, w_key, w_value, (queries, d_attended, edges), count, count
    )
    o_edge = shift(last_o[last_o.shape[0] - STRETCH :], "seq", 1)
    sent, last_core, first_back = to_send(last_grads, first_back)
    last_back = swap(sent, "tp", half)
    own_term = slot_terms(
        (first_grads[0], last_grads[0]), (first_grads[1], last_grads[1]),
        w_key, w_value, 0, slots * piece,
    )
    shares = [[own_term]] + [list(pair) for pair in zip(first_core, last_core)]
    shares.append([first_back, last_back])
    shares = [[part.reshape(-1, piece, width) for part in share] for share in shares]
    shares, o_edge = lax.optimization_barrier((shares, o_edge))
    outgoing_grads = return_grads(neighbours, me, shares, row_count, masks, capacity)
    attended = jnp.concatenate([o_edge[1:], first_o, last_o[: last_o.shape[0] - edge]], axis=0)
    totals, (flat_rows,) = exchange(outgoing_grads, masks, (flat_rows,))
    staged = stage(flat_rows, enc_gain, w_in, w_out)
    grads = encode_back(all_ids, me, enc_gain, flat_rows, staged, totals, masks)
    return (attended, grads.reshape(row_count, piece, width))


def solution(mesh):
    in_specs = (
        P(("role", "seq"), None),
        P(None, "tp"),
        P(None, "tp"),
        P(None, "tp"),
        P(),
        P(),
        P(),
        P(("role", "seq"), "tp", None),
        P(("role", "seq"), None),
        P(("role", "seq"), "tp"),
    )
    out_specs = (P(("role", "seq"), "tp"), P(("role", "seq"), "tp", None))
    return jax.shard_map(body, mesh=mesh, in_specs=in_specs, out_specs=out_specs, check_vma=False)
```

```python
import functools

import jax
import jax.numpy as jnp
from jax import lax
from jax.experimental import pallas as pl
from jax.experimental.pallas import tpu as pltpu
from jax.sharding import PartitionSpec as P

HD = 128
STRETCH = 64
EPS = 1e-06
GELU_A = 0.7978845608028654
GELU_B = 0.044715
F32 = jnp.float32
BF16 = jnp.bfloat16


def params(mib):
    return pltpu.CompilerParams(vmem_limit_bytes=mib * 1024 * 1024)


def dot(a, b):
    return jnp.dot(a, b, preferred_element_type=F32)


def dot_nt(a, b):
    return lax.dot_general(a, b, (((1,), (1,)), ((), ())), preferred_element_type=F32)


def dot_tn(a, b):
    return lax.dot_general(a, b, (((0,), (0,)), ((), ())), preferred_element_type=F32)


def whole(shape):
    return pl.BlockSpec(shape, lambda *_: (0,) * len(shape))


def smem():
    return pl.BlockSpec(memory_space=pltpu.SMEM)


def vmem():
    return pl.BlockSpec(memory_space=pltpu.VMEM)


def anywhere():
    return pl.BlockSpec(memory_space=pl.ANY)


def hbm(*arrays):
    return [pltpu.with_memory_space_constraint(array, pltpu.HBM) for array in arrays]


def tiles(size, part):
    return [(at, min(part, size - at)) for at in range(0, size, part)]


def exchange_masks(groups, peers):
    masks = range(1, groups)
    far = sorted([m for m in masks if m & (peers // 2)], reverse=True)
    near = sorted([m for m in masks if not m & (peers // 2)], key=lambda m: (m % peers != 0, -m))
    return [0, near[0], far[-1]] + far[1:-1] + near[1:-1] + [far[0], near[-1]]


def each_request(ids_ref, g, first, row_count, capacity, act):
    fan_out = ids_ref.shape[1]
    rank = jnp.int32(0)
    for s in range(ids_ref.shape[2] * fan_out):
        local = ids_ref[g, s % fan_out, s // fan_out] - first
        mine = (local >= 0) & (local < row_count)
        place = jnp.minimum(rank, capacity - 1)

        @pl.when(mine)
        def _():
            act(jnp.clip(local, 0, row_count - 1), place)

        rank = rank + mine.astype(jnp.int32)


def norm_of(x, gain):
    inverse = lax.rsqrt(jnp.mean(x * x, axis=-1, keepdims=True) + EPS)
    return (x * inverse * gain).astype(BF16), inverse


def encode_kernel(
    gain_hbm, x_hbm, w_in_hbm, w_out_hbm, enc_ref,
    gain_ref, x_ref, w_in, w_out, normed, active, sems, in_sems,
):
    rows, width = x_ref.shape
    hidden = w_in.shape[1]
    x_copy = pltpu.make_async_copy(x_hbm, x_ref, sems.at[0])
    x_copy.start()
    gain_copy = pltpu.make_async_copy(gain_hbm, gain_ref, sems.at[2])
    gain_copy.start()
    parts = [pl.ds(at, part) for at, part in tiles(hidden, hidden // 2)]
    in_copies = []
    for i, cols in enumerate(parts):
        copy = pltpu.make_async_copy(w_in_hbm.at[:, cols], w_in.at[:, cols], in_sems.at[i])
        copy.start()
        in_copies.append(copy)
    out_copy = pltpu.make_async_copy(w_out_hbm, w_out, sems.at[1])
    x_copy.wait()
    gain_copy.wait()
    normed[...], _ = norm_of(x_ref[...].astype(F32), gain_ref[...].reshape(1, width))
    for i, cols in enumerate(parts):
        in_copies[i].wait()
        if i == 0:
            out_copy.start()
        for at, part in tiles(cols.size, 256):
            band = pl.ds(cols.start + at, part)
            pre = dot(normed[...], w_in[:, band])
            tanh = jnp.tanh(GELU_A * (pre + GELU_B * (pre * pre * pre)))
            active[:, band] = (pre * (0.5 * (1.0 + tanh))).astype(BF16)
    out_copy.wait()
    for at, part in tiles(rows, 256):
        band = pl.ds(at, part)
        total = x_ref[band, :].astype(F32) + dot(active[band, :], w_out[...])
        enc_ref[band, :] = total.astype(BF16)


def encode(flat_rows, enc_gain, w_in, w_out):
    rows, width = flat_rows.shape
    hidden = w_in.shape[1]
    return pl.pallas_call(
        encode_kernel,
        in_specs=[anywhere()] * 4,
        out_specs=vmem(),
        out_shape=pltpu.VMEM((rows, width), BF16),
        scratch_shapes=[
            pltpu.VMEM((width,), F32),
            pltpu.VMEM((rows, width), BF16),
            pltpu.VMEM((width, hidden), BF16),
            pltpu.VMEM((hidden, width), BF16),
            pltpu.VMEM((rows, width), BF16),
            pltpu.VMEM((rows, hidden), BF16),
            pltpu.SemaphoreType.DMA((3,)),
            pltpu.SemaphoreType.DMA((2,)),
        ],
        compiler_params=params(14),
        cost_estimate=pl.CostEstimate(
            flops=4 * rows * width * hidden,
            bytes_accessed=4 * width * hidden + 4 * rows * width,
            transcendentals=rows * hidden,
        ),
        name="encode",
    )(*hbm(enc_gain, flat_rows, w_in, w_out))


def send_kernel(masks, ids_ref, me_ref, enc_ref, h_hbm, *refs):
    out_refs, (h_ref, h_sem, sems) = refs[:-3], refs[-3:]
    h_copy = pltpu.make_async_copy(h_hbm, h_ref, h_sem)
    h_copy.start()
    row_count = enc_ref.shape[0]
    capacity = out_refs[0].shape[0]
    me = me_ref[0]

    def copy_of(k, row, place):
        return pltpu.make_async_copy(enc_ref.at[row], out_refs[k].at[place], sems.at[k, place])

    for k, mask in enumerate(masks):
        each_request(
            ids_ref, me ^ mask, me * row_count, row_count, capacity,
            lambda row, place: copy_of(k, row, place).start(),
        )
    for k, mask in enumerate(masks):
        each_request(
            ids_ref, me ^ mask, me * row_count, row_count, capacity,
            lambda row, place: copy_of(k, row, place).wait(),
        )
    h_copy.wait()


def send_rows(all_ids, me, encoded, tokens, capacity, masks):
    row_count, piece, width = encoded.shape
    groups = all_ids.shape[0]
    return pl.pallas_call(
        functools.partial(send_kernel, masks),
        in_specs=[smem(), smem(), vmem(), anywhere()],
        out_specs=[anywhere()] * groups + [vmem()],
        out_shape=[jax.ShapeDtypeStruct((capacity, piece, width), BF16)] * groups
        + [pltpu.VMEM(tokens.shape, BF16)],
        scratch_shapes=[
            pltpu.SemaphoreType.DMA,
            pltpu.SemaphoreType.DMA((groups, capacity)),
        ],
        compiler_params=params(4),
        name="send_rows",
    )(all_ids, me, encoded, *hbm(tokens))


def stream_product(h_ref, w_hbm, first, blocks, sems, total):
    part = blocks.shape[1]
    count = h_ref.shape[1] // part // 2
    at = [first + i * part for i in range(count)]
    copies = [
        pltpu.make_async_copy(w_hbm.at[pl.ds(row, part), :], blocks.at[i % 3], sems.at[i % 3])
        for i, row in enumerate(at)
    ]
    for copy in copies[:3]:
        copy.start()
    for i, row in enumerate(at):
        copies[i].wait()
        value = dot(h_ref[:, pl.ds(row, part)], blocks[i % 3])
        total[...] = value if first + i == 0 else total[...] + value
        if i + 3 < count:
            copies[i + 3].start()


def query_first_kernel(h_ref, w_hbm, total, blocks, sems):
    stream_product(h_ref, w_hbm, 0, blocks, sems, total)


def query_last_kernel(h_ref, partial_ref, d_ref, w_hbm, out_ref, edge_ref, blocks, sems, total):
    total[...] = partial_ref[...]
    stream_product(h_ref, w_hbm, h_ref.shape[1] // 2, blocks, sems, total)
    out_ref[...] = total[...].astype(BF16)
    edge_ref[:STRETCH, :] = total[:STRETCH, :].astype(BF16)
    edge_ref[STRETCH:, :] = d_ref[:STRETCH, :]


def query_first(tokens, w_query):
    count, depth = tokens.shape
    feats = w_query.shape[1]
    return pl.pallas_call(
        query_first_kernel,
        in_specs=[vmem(), anywhere()],
        out_specs=vmem(),
        out_shape=jax.ShapeDtypeStruct((count, feats), F32),
        scratch_shapes=[pltpu.VMEM((3, 1024, feats), BF16), pltpu.SemaphoreType.DMA((3,))],
        compiler_params=params(12),
        cost_estimate=pl.CostEstimate(
            flops=count * depth * feats, bytes_accessed=depth * feats, transcendentals=0
        ),
        name="query_first",
    )(tokens, *hbm(w_query))


def query_last(tokens, partial, w_query, cotangent):
    count, depth = tokens.shape
    feats = w_query.shape[1]
    return pl.pallas_call(
        query_last_kernel,
        in_specs=[vmem()] * 3 + [anywhere()],
        out_specs=[vmem()] * 2,
        out_shape=[
            jax.ShapeDtypeStruct((count, feats), BF16),
            jax.ShapeDtypeStruct((2 * STRETCH, feats), BF16),
        ],
        scratch_shapes=[
            pltpu.VMEM((3, 1024, feats), BF16),
            pltpu.SemaphoreType.DMA((3,)),
            pltpu.VMEM((count, feats), F32),
        ],
        compiler_params=params(12),
        cost_estimate=pl.CostEstimate(
            flops=count * depth * feats, bytes_accessed=depth * feats, transcendentals=0
        ),
        name="query_last",
    )(tokens, partial, cotangent, *hbm(w_query))


def places_of(ids_ref, me, row_count, capacity):
    fan_out, stretch_count = ids_ref.shape
    ids = [ids_ref[s % fan_out, s // fan_out] for s in range(fan_out * stretch_count)]
    if row_count & (row_count - 1):
        owners = [lax.div(row, jnp.int32(row_count)) for row in ids]
    else:
        bits = jnp.int32(row_count.bit_length() - 1)
        owners = [lax.shift_right_logical(row, bits) for row in ids]
    places = []
    for s, owner in enumerate(owners):
        rank = jnp.int32(0)
        for other in owners[:s]:
            rank = rank + (other == owner).astype(jnp.int32)
        places.append((owner ^ me, jnp.minimum(rank, capacity - 1)))
    return places


def pick_kernel(row_count, masks, halves, ids_ref, me_ref, *refs):
    arrived_refs, refs = refs[: len(masks)], refs[len(masks) :]
    out_refs, sems = refs[:halves], refs[halves]
    capacity = arrived_refs[0].shape[0]
    slots = out_refs[0].shape[0]
    for s, (mask, rank) in enumerate(places_of(ids_ref, me_ref[0], row_count, capacity)):
        out_ref = out_refs[s // slots]
        for here, ref in zip(masks, arrived_refs):

            @pl.when(mask == here)
            def _():
                pltpu.make_async_copy(ref.at[rank], out_ref.at[s % slots], sems.at[s]).start()

    for s in range(slots * halves):
        out_ref = out_refs[s // slots].at[s % slots]
        pltpu.make_async_copy(arrived_refs[0].at[0], out_ref, sems.at[s]).wait()


def pick_rows(neighbours, me, arrived, row_count, masks, halves):
    capacity, piece, width = arrived[0].shape
    slots = neighbours.size
    return pl.pallas_call(
        functools.partial(pick_kernel, row_count, masks, halves),
        in_specs=[smem(), smem()] + [anywhere()] * len(arrived),
        out_specs=[anywhere()] * halves,
        out_shape=[jax.ShapeDtypeStruct((slots // halves, piece, width), BF16)] * halves,
        scratch_shapes=[pltpu.SemaphoreType.DMA((slots,))],
        compiler_params=params(4),
        name="pick_rows",
    )(neighbours, me, *arrived)


def return_kernel(row_count, masks, counts, ids_ref, me_ref, *refs):
    share_refs, refs = refs[: sum(counts)], refs[sum(counts) :]
    out_refs, (total, sems) = refs[: len(masks)], refs[len(masks) :]
    shares = []
    for count in counts:
        shares.append(share_refs[:count])
        share_refs = share_refs[count:]
    capacity = out_refs[0].shape[0]
    slots = total.shape[0]
    for s, (mask, rank) in enumerate(places_of(ids_ref, me_ref[0], row_count, capacity)):
        value = None
        for share in shares:
            each = slots // len(share)
            part = share[s // each][s % each].astype(F32)
            value = part if value is None else value + part
        total[s] = value.astype(BF16)
        for here, ref in zip(masks, out_refs):

            @pl.when(mask == here)
            def _():
                pltpu.make_async_copy(total.at[s], ref.at[rank], sems.at[s]).start()

    for s in range(slots):
        pltpu.make_async_copy(total.at[s], out_refs[0].at[0], sems.at[s]).wait()


def return_grads(neighbours, me, shares, row_count, masks, capacity):
    _, piece, width = shares[0][0].shape
    slots = neighbours.size
    groups = len(masks)
    counts = [len(share) for share in shares]
    return pl.pallas_call(
        functools.partial(return_kernel, row_count, masks, counts),
        in_specs=[smem(), smem()] + [vmem()] * sum(counts),
        out_specs=[anywhere()] * groups,
        out_shape=[jax.ShapeDtypeStruct((capacity, piece, width), BF16)] * groups,
        scratch_shapes=[
            pltpu.VMEM((slots, piece, width), BF16),
            pltpu.SemaphoreType.DMA((slots,)),
        ],
        compiler_params=params(8),
        name="return_grads",
    )(neighbours, me, *[part for share in shares for part in share])


def fill_keys(x, wk_ref, wv_ref, keys, values):
    for w_ref, out in ((wk_ref, keys), (wv_ref, values)):
        for at, part in tiles(w_ref.shape[1], 256):
            cols = pl.ds(at, part)
            out[:, cols] = dot(x, w_ref[:, cols]).astype(BF16)


def project_kernel(count, *refs):
    piece_refs, (wk_ref, wv_ref, *out_refs) = refs[: -4 - 2 * count], refs[-4 - 2 * count :]
    each = len(piece_refs) // count
    for i in range(count):
        x = [ref[...] for ref in piece_refs[i * each : (i + 1) * each]]
        x = jnp.concatenate(x, axis=0)
        fill_keys(x, wk_ref, wv_ref, out_refs[2 * i], out_refs[2 * i + 1])
    for w_ref, out in ((wk_ref, out_refs[-2]), (wv_ref, out_refs[-1])):
        for at, part in tiles(w_ref.shape[1], 256):
            out[pl.ds(at, part), :] = w_ref[:, pl.ds(at, part)].T


def project(halves, w_key, w_value):
    pieces = [piece for half in halves for piece in half]
    rows, width = pieces[0].shape
    rows *= len(halves[0])
    feats = w_key.shape[1]
    count = len(halves)
    out = pl.pallas_call(
        functools.partial(project_kernel, count),
        in_specs=[vmem()] * (len(pieces) + 2),
        out_specs=[vmem()] * (2 * count + 2),
        out_shape=[jax.ShapeDtypeStruct((rows, feats), BF16)] * (2 * count)
        + [jax.ShapeDtypeStruct((feats, width), BF16)] * 2,
        compiler_params=params(16),
        cost_estimate=pl.CostEstimate(
            flops=4 * count * rows * width * feats,
            bytes_accessed=4 * width * feats + 2 * count * rows * (width + 2 * feats),
            transcendentals=0,
        ),
        name="project",
    )(*pieces, w_key, w_value)
    return [out[2 * i : 2 * i + 2] for i in range(count)], out[2 * count :]


def two_blocks(value):
    zeros = jnp.zeros((value.shape[0], HD), value.dtype)
    top = jnp.concatenate([value[:, :HD], zeros], axis=1)
    low = jnp.concatenate([zeros, value[:, HD:]], axis=1)
    return jnp.concatenate([top, low], axis=0)


def moved_up(rows, by):
    return pltpu.roll(rows.astype(F32), rows.shape[0] - by, 0)


def attend_kernel(far_count, first, count, has_edges, *refs):
    near_refs, far_refs, refs = refs[:2], refs[2 : 2 + far_count], refs[2 + far_count :]
    weight_refs, token_refs, refs = refs[:2], refs[2 : 4 + has_edges], refs[4 + has_edges :]
    att_ref, near_dk, near_dv, far_dk, far_dv, far_k, far_v, block_q, block_d = refs
    x = jnp.concatenate([ref[...] for ref in far_refs], axis=0)
    fill_keys(x, *weight_refs, far_k, far_v)
    rows = far_refs[0].shape[0]
    part = rows // count
    block = STRETCH
    for i, out in enumerate((block_q, block_d)):
        own = token_refs[i]
        begin = first * block + block - 16
        size = own.shape[0] - begin if has_edges else count * block + 16
        for at, wide in tiles(own.shape[1], 256):
            cols = pl.ds(at, wide)
            values = own[pl.ds(begin, size), cols]
            if has_edges:
                edge = token_refs[2][pl.ds(i * block, block), cols]
                values = jnp.concatenate([values, edge], axis=0)
            out[:, cols] = moved_up(values, 15)[: count * block].astype(BF16)
    scale = HD ** (-0.5)

    def bands(near, far, c):
        at = [(ref, i) for ref in (near, far) for i in range(far_count)]
        return [(ref, pl.ds(pl.multiple_of(i * rows + c * part, part), part)) for ref, i in at]

    def stretch(c, carry):
        mine = pl.ds(pl.multiple_of(c * block, block), block)
        heads = [pl.ds(h, 2 * HD) for h in range(0, block_q.shape[1], 2 * HD)]
        for at in range(0, len(heads), 2):
            pairs = []
            for cols in heads[at : at + 2]:
                here = [bands(near_refs[0], far_k, c), bands(near_refs[1], far_v, c)]
                k, v = (jnp.concatenate([ref[b, cols] for ref, b in pair], axis=0) for pair in here)
                q, d = two_blocks(block_q[mine, cols]), two_blocks(block_d[mine, cols])
                pairs.append((cols, v, q, d, dot_nt(k, q) * scale, dot_nt(v, d)))
            sums = []
            for cols, v, q, d, scores, dprobs in pairs:
                weights = jnp.exp(scores - jnp.max(scores, axis=0, keepdims=True))
                probability = weights * (1.0 / jnp.sum(weights, axis=0, keepdims=True))
                centre = jnp.sum(probability * dprobs, axis=0, keepdims=True)
                dscores = (probability * (dprobs - centre)).astype(BF16)
                sums.append((cols, v, q, d, probability.astype(BF16), dscores))
            for cols, v, q, d, rounded, dscores in sums:
                out = dot_tn(rounded, v)
                att_ref[mine, cols] = jnp.concatenate(
                    [out[:block, :HD], out[block:, HD:]], axis=1
                ).astype(BF16)
                value_grads = dot(rounded, d).astype(BF16)
                key_grads = (dot(dscores, q) * scale).astype(BF16)
                for i, (ref, b) in enumerate(bands(near_dk, far_dk, c)):
                    ref[b, cols] = key_grads[i * part : (i + 1) * part]
                for i, (ref, b) in enumerate(bands(near_dv, far_dv, c)):
                    ref[b, cols] = value_grads[i * part : (i + 1) * part]
        return carry

    lax.fori_loop(0, count, stretch, 0)


def attend(near, far, w_key, w_value, tokens, first, count):
    width, feats = w_key.shape
    rows = near[0].shape[0]
    return pl.pallas_call(
        functools.partial(attend_kernel, len(far), first, count, len(tokens) - 2),
        in_specs=[vmem()] * (4 + len(far) + len(tokens)),
        out_specs=[vmem()] * 5,
        out_shape=[jax.ShapeDtypeStruct((count * STRETCH, feats), BF16)]
        + [jax.ShapeDtypeStruct((rows, feats), BF16)] * 4,
        scratch_shapes=[pltpu.VMEM((rows, feats), BF16)] * 2
        + [pltpu.VMEM((count * STRETCH, feats), BF16)] * 2,
        compiler_params=params(20),
        cost_estimate=pl.CostEstimate(
            flops=4 * rows * width * feats + 40 * rows * STRETCH * feats,
            bytes_accessed=4 * width * feats + 12 * rows * feats,
            transcendentals=2 * rows * STRETCH * feats // HD,
        ),
        name="attend",
    )(*near, *far, w_key, w_value, *tokens)


def terms_kernel(numbers, *refs):
    count = len(numbers)
    grad_refs, (wk_ref, wv_ref), term_refs = refs[: 2 * count], refs[2 * count : -count], refs[-count:]
    rows = term_refs[0].shape[0]

    def rows_of(refs):
        parts = [ref[pl.ds(number * rows, rows), :] for number, ref in zip(numbers, refs)]
        return jnp.concatenate(parts, axis=0)

    term = dot(rows_of(grad_refs[:count]), wk_ref[...])
    term = term + dot(rows_of(grad_refs[count:]), wv_ref[...])
    term = term.astype(BF16)
    for i, ref in enumerate(term_refs):
        ref[...] = term[i * rows : (i + 1) * rows]


def slot_terms(asked, turned, rows):
    feats, width = turned[0].shape
    count = len(asked)
    return pl.pallas_call(
        functools.partial(terms_kernel, [number for _, _, number in asked]),
        in_specs=[vmem()] * (2 * count + 2),
        out_specs=[vmem()] * count,
        out_shape=[jax.ShapeDtypeStruct((rows, width), BF16)] * count,
        compiler_params=params(20),
        cost_estimate=pl.CostEstimate(
            flops=4 * count * rows * width * feats,
            bytes_accessed=4 * width * feats + 2 * count * rows * (width + 2 * feats),
            transcendentals=0,
        ),
        name="slot_terms",
    )(*[keys for keys, _, _ in asked], *[values for _, values, _ in asked], *turned)


def stage_kernel(
    gain_ref, x_ref, w_in_ref, w_out_ref, inv_ref, slope_ref, w_in_turned, w_out_turned, normed
):
    rows, width = x_ref.shape
    normed[...], inv_ref[...] = norm_of(
        x_ref[...].astype(F32), gain_ref[...].reshape(1, width)
    )
    for at, part in tiles(w_in_ref.shape[1], 256):
        cols = pl.ds(at, part)
        pre = dot(normed[...], w_in_ref[:, cols])
        square = pre * pre
        tanh = jnp.tanh(GELU_A * pre * (1.0 + GELU_B * square))
        slope_ref[:, cols] = 0.5 * (1.0 + tanh) + 0.5 * pre * (1.0 - tanh * tanh) * (
            GELU_A * (1.0 + 3.0 * GELU_B * square)
        )
        w_in_turned[cols, :] = w_in_ref[:, cols].T
        w_out_turned[:, cols] = w_out_ref[cols, :].T


def stage(flat_rows, enc_gain, w_in, w_out):
    rows, width = flat_rows.shape
    hidden = w_in.shape[1]
    return pl.pallas_call(
        stage_kernel,
        in_specs=[vmem()] * 4,
        out_specs=[vmem()] * 4,
        out_shape=[
            jax.ShapeDtypeStruct((rows, 1), F32),
            jax.ShapeDtypeStruct((rows, hidden), F32),
            jax.ShapeDtypeStruct((hidden, width), BF16),
            jax.ShapeDtypeStruct((width, hidden), BF16),
        ],
        scratch_shapes=[pltpu.VMEM((rows, width), BF16)],
        compiler_params=params(24),
        cost_estimate=pl.CostEstimate(
            flops=2 * rows * width * hidden,
            bytes_accessed=8 * width * hidden + 4 * rows * hidden + 4 * rows * width,
            transcendentals=rows * hidden,
        ),
        name="stage",
    )(enc_gain, flat_rows, w_in, w_out)


def encode_back_kernel(
    masks, ids_ref, me_ref, gain_ref, x_ref, inv_ref, slope_ref, w_in_turned, w_out_turned, *refs
):
    arrived_refs, (out_ref, row_grad, upstream, d_pre) = refs[:-4], refs[-4:]
    capacity, piece, width = arrived_refs[0].shape
    row_count = row_grad.shape[0]
    rows = x_ref.shape[0]
    row_grad[...] = jnp.zeros_like(row_grad)
    me = me_ref[0]
    for mask, ref in zip(masks, arrived_refs):

        def add(row, place):
            row_grad[row] += ref[place].astype(F32)

        each_request(ids_ref, me ^ mask, me * row_count, row_count, capacity, add)
    upstream[...] = row_grad[...].reshape(upstream.shape).astype(BF16)
    for at, part in tiles(w_out_turned.shape[1], 256):
        cols = pl.ds(at, part)
        d_act = dot(upstream[...], w_out_turned[:, cols])
        d_pre[:, cols] = (d_act * slope_ref[:, cols]).astype(BF16)
    gain = gain_ref[...].reshape(1, width)
    for at, part in tiles(rows, 256):
        band = pl.ds(at, part)
        scaled = dot(d_pre[band, :], w_in_turned[...]) * gain
        x = x_ref[band, :].astype(F32)
        inverse = inv_ref[band, :]
        mean = jnp.mean(scaled * x, axis=-1, keepdims=True)
        back = inverse * scaled - x * (inverse * inverse * inverse * mean)
        summed = row_grad[at // piece : (at + part) // piece].reshape(part, width)
        out_ref[band, :] = (summed + back).astype(BF16)


def encode_back(all_ids, me, enc_gain, flat_rows, staged, arrived, masks):
    rows, hidden = staged[1].shape
    _, piece, width = arrived[0].shape
    return pl.pallas_call(
        functools.partial(encode_back_kernel, masks),
        in_specs=[smem(), smem()] + [vmem()] * (6 + len(arrived)),
        out_specs=vmem(),
        out_shape=jax.ShapeDtypeStruct((rows, width), BF16),
        scratch_shapes=[
            pltpu.VMEM((rows // piece, piece, width), F32),
            pltpu.VMEM((rows, width), BF16),
            pltpu.VMEM((rows, hidden), BF16),
        ],
        compiler_params=params(28),
        cost_estimate=pl.CostEstimate(
            flops=4 * rows * width * hidden,
            bytes_accessed=4 * width * hidden + 4 * rows * hidden + 8 * rows * width,
            transcendentals=0,
        ),
        name="encode_back",
    )(all_ids, me, enc_gain, flat_rows, *staged, *arrived)


def shift(value, axis, by):
    peers = lax.axis_size(axis)
    pairs = [(i, i + by) for i in range(peers) if 0 <= i + by < peers]
    return lax.ppermute(value, axis, pairs)


def swap(value, axis, bit):
    return lax.ppermute(value, axis, [(i, i ^ bit) for i in range(lax.axis_size(axis))])


def exchange(buffers, masks, later, between=None):
    axes = ("role", "seq")
    count = len(buffers)
    arrived = [buffers[0]] + [swap(buffers[k], axes, masks[k]) for k in range(1, count - 2)]
    for early, k in ((1, count - 2), (2, count - 1)):
        arrived[early], value, later = lax.optimization_barrier((arrived[early], buffers[k], later))
        arrived.append(swap(value, axes, masks[k]))
        if early == 1 and between is not None:
            later = between(later)
    return arrived, later


def add_up(shares):
    if len(shares) == 1:
        return shares[0]
    return functools.reduce(jnp.add, [share.astype(F32) for share in shares]).astype(BF16)


def body(hidden, w_query, w_key, w_value, enc_gain, w_in, w_out, db_states, neighbours, d_attended):
    groups = lax.axis_size(("role", "seq"))
    shards = lax.axis_size("tp")
    me = lax.axis_index(("role", "seq")).astype(jnp.int32).reshape(1)
    masks = exchange_masks(groups, lax.axis_size("seq"))
    row_count, piece, width = db_states.shape
    stretch_count, fan_out = neighbours.shape
    slots = stretch_count * fan_out
    tokens = hidden.shape[0]
    edge = STRETCH - 1
    capacity = max(2, 2 * ((stretch_count - 1 + groups - 2) // (groups - 1)))
    neighbours = neighbours.T
    all_ids = lax.all_to_all(
        jnp.broadcast_to(neighbours[None], (groups, fan_out, stretch_count)),
        ("role", "seq"), 0, 0, tiled=True,
    )
    flat_rows = db_states.reshape(row_count * piece, width)
    encoded = encode(flat_rows, enc_gain, w_in, w_out)
    *outgoing, hidden = send_rows(
        all_ids, me, encoded.reshape(row_count, piece, width), hidden, capacity, masks
    )
    arrived, (partial, hidden) = exchange(
        outgoing, masks, hidden, lambda tokens: (query_first(tokens, w_query), tokens)
    )
    queries, edges = query_last(hidden, partial, w_query, d_attended)
    queries, neighbours = lax.optimization_barrier((queries, neighbours))
    count = stretch_count // 2
    first_own, last_own = [
        value.reshape(slots * piece // 2, width)
        for value in pick_rows(neighbours, me, arrived, row_count, masks, 2)
    ]
    first_own, edges = lax.optimization_barrier((first_own, edges))
    edges = shift(edges, "seq", -1)
    bits = [1 << i for i in range(shards.bit_length() - 1)]
    half = shards // 2

    def gathered(pieces):
        for bit in reversed(bits[:-1]):
            pieces.update({mask | bit: swap(pieces[mask], "tp", bit) for mask in list(pieces)})
        return [pieces[mask] for mask in sorted(pieces)]

    first_far = swap(first_own, "tp", half)
    first_near = gathered({0: first_own})
    last_far = swap(last_own, "tp", half)
    last_near = gathered({0: last_own})
    (first_kv, last_kv), turned = project([first_near, last_near], w_key, w_value)
    first_far, first_kv, last_kv = lax.optimization_barrier((first_far, first_kv, last_kv))
    first_far = gathered({half: first_far})
    first_far[-1], edges = lax.optimization_barrier((first_far[-1], edges))
    first_o, *first_grads = attend(
        first_kv, first_far, w_key, w_value, (queries, d_attended), 0, count
    )
    first_o, last_far = lax.optimization_barrier((first_o, last_far))
    last_far = gathered({half: last_far})

    rows = slots * piece // 2

    def fold(shares):
        for bit in bits[:-1]:
            for mask in sorted([mask for mask in shares if mask & bit], reverse=True):
                shares[mask ^ bit].append(swap(add_up(shares.pop(mask)), "tp", bit))
        return shares[0]

    def to_send(grads, others, tied):
        numbers = list(reversed(range(1, half)))
        asked = [(grads[2], grads[3], j) for j in numbers]
        asked += [(each[0], each[1], j) for each in others for j in numbers]
        terms = slot_terms(asked, turned, rows)
        sums = []
        for i in range(1 + len(others)):
            mine = terms[i * len(numbers) : (i + 1) * len(numbers)]
            sums.append({0: [], **{j: [term] for j, term in zip(numbers, mine)}})
        tied, grads = lax.optimization_barrier((tied, grads))
        sums[0][0] = list(slot_terms([(grads[2], grads[3], 0)], turned, rows))
        far, *near = [fold(shares) for shares in sums]
        return add_up(far), near, tied

    sent, _, edges = to_send(first_grads, [], edges)
    sent, edges = lax.optimization_barrier((sent, edges))
    first_back = swap(sent, "tp", half)
    last_o, *last_grads = attend(
        last_kv, last_far, w_key, w_value, (queries, d_attended, edges), count, count
    )
    o_edge = shift(last_o[last_o.shape[0] - STRETCH :], "seq", 1)
    sent, near_back, first_back = to_send(last_grads, [first_grads, last_grads], first_back)
    last_back = swap(sent, "tp", half)
    own_terms = slot_terms(
        [(grads[0], grads[1], 0) for grads in (first_grads, last_grads)], turned, rows
    )
    shares = [list(own_terms)] + [list(pair) for pair in zip(*near_back)]
    shares.append([first_back, last_back])
    shares = [[part.reshape(-1, piece, width) for part in share] for share in shares]
    outgoing_grads = return_grads(neighbours, me, shares, row_count, masks, capacity)
    attended = jnp.concatenate([o_edge[1:], first_o, last_o[: last_o.shape[0] - edge]], axis=0)
    totals, flat_rows = exchange(outgoing_grads, masks, flat_rows)
    staged = stage(flat_rows, enc_gain, w_in, w_out)
    grads = encode_back(all_ids, me, enc_gain, flat_rows, staged, totals, masks)
    return (attended, grads.reshape(row_count, piece, width))


def solution(mesh):
    in_specs = (
        P(("role", "seq"), None),
        P(None, "tp"),
        P(None, "tp"),
        P(None, "tp"),
        P(),
        P(),
        P(),
        P(("role", "seq"), "tp", None),
        P(("role", "seq"), None),
        P(("role", "seq"), "tp"),
    )
    out_specs = (P(("role", "seq"), "tp"), P(("role", "seq"), "tp", None))
    return jax.shard_map(body, mesh=mesh, in_specs=in_specs, out_specs=out_specs, check_vma=False)
```

```python
import functools

import jax
import jax.numpy as jnp
from jax import lax
from jax.experimental import pallas as pl
from jax.experimental.pallas import tpu as pltpu
from jax.sharding import PartitionSpec as P

HD = 128
STRETCH = 64
EPS = 1e-06
GELU_A = 0.7978845608028654
GELU_B = 0.044715
F32 = jnp.float32
BF16 = jnp.bfloat16


def params(mib):
    return pltpu.CompilerParams(vmem_limit_bytes=mib * 1024 * 1024)


def dot(a, b):
    return jnp.dot(a, b, preferred_element_type=F32)


def dot_nt(a, b):
    return lax.dot_general(a, b, (((1,), (1,)), ((), ())), preferred_element_type=F32)


def dot_tn(a, b):
    return lax.dot_general(a, b, (((0,), (0,)), ((), ())), preferred_element_type=F32)


def whole(shape):
    return pl.BlockSpec(shape, lambda *_: (0,) * len(shape))


def smem():
    return pl.BlockSpec(memory_space=pltpu.SMEM)


def vmem():
    return pl.BlockSpec(memory_space=pltpu.VMEM)


def anywhere():
    return pl.BlockSpec(memory_space=pl.ANY)


def hbm(*arrays):
    return [pltpu.with_memory_space_constraint(array, pltpu.HBM) for array in arrays]


def tiles(size, part):
    return [(at, min(part, size - at)) for at in range(0, size, part)]


def exchange_masks(groups, peers):
    masks = range(1, groups)
    far = sorted([m for m in masks if m & (peers // 2)], reverse=True)
    near = sorted([m for m in masks if not m & (peers // 2)], key=lambda m: (m % peers != 0, -m))
    return [0, near[0], far[-1]] + far[1:-1] + near[1:-1] + [far[0], near[-1]]


def each_request(ids_ref, g, first, row_count, capacity, act):
    fan_out = ids_ref.shape[1]
    rank = jnp.int32(0)
    for s in range(ids_ref.shape[2] * fan_out):
        local = ids_ref[g, s % fan_out, s // fan_out] - first
        mine = (local >= 0) & (local < row_count)
        place = jnp.minimum(rank, capacity - 1)

        @pl.when(mine)
        def _():
            act(jnp.clip(local, 0, row_count - 1), place)

        rank = rank + mine.astype(jnp.int32)


def norm_of(x, gain):
    inverse = lax.rsqrt(jnp.mean(x * x, axis=-1, keepdims=True) + EPS)
    return (x * inverse * gain).astype(BF16), inverse


def encode_kernel(
    gain_hbm, x_hbm, w_in_hbm, w_out_hbm, enc_ref,
    gain_ref, x_ref, w_in, w_out, normed, active, sems, in_sems,
):
    rows, width = x_ref.shape
    hidden = w_in.shape[1]
    x_copy = pltpu.make_async_copy(x_hbm, x_ref, sems.at[0])
    x_copy.start()
    gain_copy = pltpu.make_async_copy(gain_hbm, gain_ref, sems.at[2])
    gain_copy.start()
    parts = [pl.ds(at, part) for at, part in tiles(hidden, hidden // 2)]
    in_copies = []
    for i, cols in enumerate(parts):
        copy = pltpu.make_async_copy(w_in_hbm.at[:, cols], w_in.at[:, cols], in_sems.at[i])
        copy.start()
        in_copies.append(copy)
    out_copy = pltpu.make_async_copy(w_out_hbm, w_out, sems.at[1])
    x_copy.wait()
    gain_copy.wait()
    normed[...], _ = norm_of(x_ref[...].astype(F32), gain_ref[...].reshape(1, width))
    for i, cols in enumerate(parts):
        in_copies[i].wait()
        if i == 0:
            out_copy.start()
        for at, part in tiles(cols.size, 256):
            band = pl.ds(cols.start + at, part)
            pre = dot(normed[...], w_in[:, band])
            tanh = jnp.tanh(GELU_A * (pre + GELU_B * (pre * pre * pre)))
            active[:, band] = (pre * (0.5 * (1.0 + tanh))).astype(BF16)
    out_copy.wait()
    for at, part in tiles(rows, 256):
        band = pl.ds(at, part)
        total = x_ref[band, :].astype(F32) + dot(active[band, :], w_out[...])
        enc_ref[band, :] = total.astype(BF16)


def encode(flat_rows, enc_gain, w_in, w_out):
    rows, width = flat_rows.shape
    hidden = w_in.shape[1]
    return pl.pallas_call(
        encode_kernel,
        in_specs=[anywhere()] * 4,
        out_specs=vmem(),
        out_shape=pltpu.VMEM((rows, width), BF16),
        scratch_shapes=[
            pltpu.VMEM((width,), F32),
            pltpu.VMEM((rows, width), BF16),
            pltpu.VMEM((width, hidden), BF16),
            pltpu.VMEM((hidden, width), BF16),
            pltpu.VMEM((rows, width), BF16),
            pltpu.VMEM((rows, hidden), BF16),
            pltpu.SemaphoreType.DMA((3,)),
            pltpu.SemaphoreType.DMA((2,)),
        ],
        compiler_params=params(14),
        cost_estimate=pl.CostEstimate(
            flops=4 * rows * width * hidden,
            bytes_accessed=4 * width * hidden + 4 * rows * width,
            transcendentals=rows * hidden,
        ),
        name="encode",
    )(*hbm(enc_gain, flat_rows, w_in, w_out))


def send_kernel(masks, ids_ref, me_ref, enc_ref, h_hbm, *refs):
    out_refs, (h_ref, h_sem, sems) = refs[:-3], refs[-3:]
    h_copy = pltpu.make_async_copy(h_hbm, h_ref, h_sem)
    h_copy.start()
    row_count = enc_ref.shape[0]
    capacity = out_refs[0].shape[0]
    me = me_ref[0]

    def copy_of(k, row, place):
        return pltpu.make_async_copy(enc_ref.at[row], out_refs[k].at[place], sems.at[k, place])

    for k, mask in enumerate(masks):
        each_request(
            ids_ref, me ^ mask, me * row_count, row_count, capacity,
            lambda row, place: copy_of(k, row, place).start(),
        )
    for k, mask in enumerate(masks):
        each_request(
            ids_ref, me ^ mask, me * row_count, row_count, capacity,
            lambda row, place: copy_of(k, row, place).wait(),
        )
    h_copy.wait()


def send_rows(all_ids, me, encoded, tokens, capacity, masks):
    row_count, piece, width = encoded.shape
    groups = all_ids.shape[0]
    return pl.pallas_call(
        functools.partial(send_kernel, masks),
        in_specs=[smem(), smem(), vmem(), anywhere()],
        out_specs=[anywhere()] * groups + [vmem()],
        out_shape=[jax.ShapeDtypeStruct((capacity, piece, width), BF16)] * groups
        + [pltpu.VMEM(tokens.shape, BF16)],
        scratch_shapes=[
            pltpu.SemaphoreType.DMA,
            pltpu.SemaphoreType.DMA((groups, capacity)),
        ],
        compiler_params=params(4),
        name="send_rows",
    )(all_ids, me, encoded, *hbm(tokens))


def stream_product(h_ref, w_hbm, first, blocks, sems, total):
    part = blocks.shape[1]
    count = h_ref.shape[1] // part // 2
    at = [first + i * part for i in range(count)]
    copies = [
        pltpu.make_async_copy(w_hbm.at[pl.ds(row, part), :], blocks.at[i % 3], sems.at[i % 3])
        for i, row in enumerate(at)
    ]
    for copy in copies[:3]:
        copy.start()
    for i, row in enumerate(at):
        copies[i].wait()
        value = dot(h_ref[:, pl.ds(row, part)], blocks[i % 3])
        total[...] = value if first + i == 0 else total[...] + value
        if i + 3 < count:
            copies[i + 3].start()


def query_first_kernel(h_ref, w_hbm, total, blocks, sems):
    stream_product(h_ref, w_hbm, 0, blocks, sems, total)


def query_last_kernel(h_ref, partial_ref, d_ref, w_hbm, out_ref, edge_ref, blocks, sems, total):
    total[...] = partial_ref[...]
    stream_product(h_ref, w_hbm, h_ref.shape[1] // 2, blocks, sems, total)
    out_ref[...] = total[...].astype(BF16)
    edge_ref[:STRETCH, :] = total[:STRETCH, :].astype(BF16)
    edge_ref[STRETCH:, :] = d_ref[:STRETCH, :]


def query_first(tokens, w_query):
    count, depth = tokens.shape
    feats = w_query.shape[1]
    return pl.pallas_call(
        query_first_kernel,
        in_specs=[vmem(), anywhere()],
        out_specs=vmem(),
        out_shape=jax.ShapeDtypeStruct((count, feats), F32),
        scratch_shapes=[pltpu.VMEM((3, 1024, feats), BF16), pltpu.SemaphoreType.DMA((3,))],
        compiler_params=params(12),
        cost_estimate=pl.CostEstimate(
            flops=count * depth * feats, bytes_accessed=depth * feats, transcendentals=0
        ),
        name="query_first",
    )(tokens, *hbm(w_query))


def query_last(tokens, partial, w_query, cotangent):
    count, depth = tokens.shape
    feats = w_query.shape[1]
    return pl.pallas_call(
        query_last_kernel,
        in_specs=[vmem()] * 3 + [anywhere()],
        out_specs=[vmem()] * 2,
        out_shape=[
            jax.ShapeDtypeStruct((count, feats), BF16),
            jax.ShapeDtypeStruct((2 * STRETCH, feats), BF16),
        ],
        scratch_shapes=[
            pltpu.VMEM((3, 1024, feats), BF16),
            pltpu.SemaphoreType.DMA((3,)),
            pltpu.VMEM((count, feats), F32),
        ],
        compiler_params=params(12),
        cost_estimate=pl.CostEstimate(
            flops=count * depth * feats, bytes_accessed=depth * feats, transcendentals=0
        ),
        name="query_last",
    )(tokens, partial, cotangent, *hbm(w_query))


def places_of(ids_ref, me, row_count, capacity):
    fan_out, stretch_count = ids_ref.shape
    ids = [ids_ref[s % fan_out, s // fan_out] for s in range(fan_out * stretch_count)]
    if row_count & (row_count - 1):
        owners = [lax.div(row, jnp.int32(row_count)) for row in ids]
    else:
        bits = jnp.int32(row_count.bit_length() - 1)
        owners = [lax.shift_right_logical(row, bits) for row in ids]
    places = []
    for s, owner in enumerate(owners):
        rank = jnp.int32(0)
        for other in owners[:s]:
            rank = rank + (other == owner).astype(jnp.int32)
        places.append((owner ^ me, jnp.minimum(rank, capacity - 1)))
    return places


def pick_kernel(row_count, masks, halves, ids_ref, me_ref, *refs):
    arrived_refs, refs = refs[: len(masks)], refs[len(masks) :]
    out_refs, sems = refs[:halves], refs[halves]
    capacity = arrived_refs[0].shape[0]
    slots = out_refs[0].shape[0]
    for s, (mask, rank) in enumerate(places_of(ids_ref, me_ref[0], row_count, capacity)):
        out_ref = out_refs[s // slots]
        for here, ref in zip(masks, arrived_refs):

            @pl.when(mask == here)
            def _():
                pltpu.make_async_copy(ref.at[rank], out_ref.at[s % slots], sems.at[s]).start()

    for s in range(slots * halves):
        out_ref = out_refs[s // slots].at[s % slots]
        pltpu.make_async_copy(arrived_refs[0].at[0], out_ref, sems.at[s]).wait()


def pick_rows(neighbours, me, arrived, row_count, masks, halves):
    capacity, piece, width = arrived[0].shape
    slots = neighbours.size
    return pl.pallas_call(
        functools.partial(pick_kernel, row_count, masks, halves),
        in_specs=[smem(), smem()] + [anywhere()] * len(arrived),
        out_specs=[anywhere()] * halves,
        out_shape=[jax.ShapeDtypeStruct((slots // halves, piece, width), BF16)] * halves,
        scratch_shapes=[pltpu.SemaphoreType.DMA((slots,))],
        compiler_params=params(4),
        name="pick_rows",
    )(neighbours, me, *arrived)


def return_kernel(row_count, masks, counts, ids_ref, me_ref, *refs):
    share_refs, refs = refs[: sum(counts)], refs[sum(counts) :]
    out_refs, (total, sems) = refs[: len(masks)], refs[len(masks) :]
    shares = []
    for count in counts:
        shares.append(share_refs[:count])
        share_refs = share_refs[count:]
    capacity = out_refs[0].shape[0]
    slots = total.shape[0]
    for s, (mask, rank) in enumerate(places_of(ids_ref, me_ref[0], row_count, capacity)):
        value = None
        for share in shares:
            each = slots // len(share)
            part = share[s // each][s % each].astype(F32)
            value = part if value is None else value + part
        total[s] = value.astype(BF16)
        for here, ref in zip(masks, out_refs):

            @pl.when(mask == here)
            def _():
                pltpu.make_async_copy(total.at[s], ref.at[rank], sems.at[s]).start()

    for s in range(slots):
        pltpu.make_async_copy(total.at[s], out_refs[0].at[0], sems.at[s]).wait()


def return_grads(neighbours, me, shares, row_count, masks, capacity):
    _, piece, width = shares[0][0].shape
    slots = neighbours.size
    groups = len(masks)
    counts = [len(share) for share in shares]
    return pl.pallas_call(
        functools.partial(return_kernel, row_count, masks, counts),
        in_specs=[smem(), smem()] + [vmem()] * sum(counts),
        out_specs=[anywhere()] * groups,
        out_shape=[jax.ShapeDtypeStruct((capacity, piece, width), BF16)] * groups,
        scratch_shapes=[
            pltpu.VMEM((slots, piece, width), BF16),
            pltpu.SemaphoreType.DMA((slots,)),
        ],
        compiler_params=params(8),
        name="return_grads",
    )(neighbours, me, *[part for share in shares for part in share])


def fill_keys(x, wk_ref, wv_ref, keys, values):
    for w_ref, out in ((wk_ref, keys), (wv_ref, values)):
        for at, part in tiles(w_ref.shape[1], 256):
            cols = pl.ds(at, part)
            out[:, cols] = dot(x, w_ref[:, cols]).astype(BF16)


def project_kernel(count, *refs):
    piece_refs, (wk_ref, wv_ref, *out_refs) = refs[: -4 - 2 * count], refs[-4 - 2 * count :]
    each = len(piece_refs) // count
    for i in range(count):
        x = [ref[...] for ref in piece_refs[i * each : (i + 1) * each]]
        x = jnp.concatenate(x, axis=0)
        fill_keys(x, wk_ref, wv_ref, out_refs[2 * i], out_refs[2 * i + 1])
    for w_ref, out in ((wk_ref, out_refs[-2]), (wv_ref, out_refs[-1])):
        for at, part in tiles(w_ref.shape[1], 256):
            out[pl.ds(at, part), :] = w_ref[:, pl.ds(at, part)].T


def project(halves, w_key, w_value):
    pieces = [piece for half in halves for piece in half]
    rows, width = pieces[0].shape
    rows *= len(halves[0])
    feats = w_key.shape[1]
    count = len(halves)
    out = pl.pallas_call(
        functools.partial(project_kernel, count),
        in_specs=[vmem()] * (len(pieces) + 2),
        out_specs=[vmem()] * (2 * count + 2),
        out_shape=[jax.ShapeDtypeStruct((rows, feats), BF16)] * (2 * count)
        + [jax.ShapeDtypeStruct((feats, width), BF16)] * 2,
        compiler_params=params(16),
        cost_estimate=pl.CostEstimate(
            flops=4 * count * rows * width * feats,
            bytes_accessed=4 * width * feats + 2 * count * rows * (width + 2 * feats),
            transcendentals=0,
        ),
        name="project",
    )(*pieces, w_key, w_value)
    return [out[2 * i : 2 * i + 2] for i in range(count)], out[2 * count :]


def two_blocks(value):
    zeros = jnp.zeros((value.shape[0], HD), value.dtype)
    top = jnp.concatenate([value[:, :HD], zeros], axis=1)
    low = jnp.concatenate([zeros, value[:, HD:]], axis=1)
    return jnp.concatenate([top, low], axis=0)


def moved_up(rows, by):
    return pltpu.roll(rows.astype(F32), rows.shape[0] - by, 0)


def attend_kernel(far_count, first, count, has_edges, *refs):
    near_refs, far_refs, refs = refs[:2], refs[2 : 2 + far_count], refs[2 + far_count :]
    weight_refs, token_refs, refs = refs[:2], refs[2 : 4 + has_edges], refs[4 + has_edges :]
    att_ref, near_dk, near_dv, far_dk, far_dv, far_k, far_v, block_q, block_d = refs
    x = jnp.concatenate([ref[...] for ref in far_refs], axis=0)
    fill_keys(x, *weight_refs, far_k, far_v)
    rows = far_refs[0].shape[0]
    part = rows // count
    block = STRETCH
    for i, out in enumerate((block_q, block_d)):
        own = token_refs[i]
        begin = first * block + block - 16
        size = own.shape[0] - begin if has_edges else count * block + 16
        for at, wide in tiles(own.shape[1], 256):
            cols = pl.ds(at, wide)
            values = own[pl.ds(begin, size), cols]
            if has_edges:
                edge = token_refs[2][pl.ds(i * block, block), cols]
                values = jnp.concatenate([values, edge], axis=0)
            out[:, cols] = moved_up(values, 15)[: count * block].astype(BF16)
    scale = HD ** (-0.5)

    def bands(near, far, c):
        at = [(ref, i) for ref in (near, far) for i in range(far_count)]
        return [(ref, pl.ds(pl.multiple_of(i * rows + c * part, part), part)) for ref, i in at]

    def stretch(c, carry):
        mine = pl.ds(pl.multiple_of(c * block, block), block)
        heads = [pl.ds(h, 2 * HD) for h in range(0, block_q.shape[1], 2 * HD)]
        for at in range(0, len(heads), 4):
            pairs = []
            for cols in heads[at : at + 4]:
                here = [bands(near_refs[0], far_k, c), bands(near_refs[1], far_v, c)]
                k, v = (jnp.concatenate([ref[b, cols] for ref, b in pair], axis=0) for pair in here)
                q, d = two_blocks(block_q[mine, cols]), two_blocks(block_d[mine, cols])
                pairs.append((cols, v, q, d, dot_nt(k, q) * scale, dot_nt(v, d)))
            sums = []
            for cols, v, q, d, scores, dprobs in pairs:
                weights = jnp.exp(scores - jnp.max(scores, axis=0, keepdims=True))
                probability = weights * (1.0 / jnp.sum(weights, axis=0, keepdims=True))
                centre = jnp.sum(probability * dprobs, axis=0, keepdims=True)
                dscores = (probability * (dprobs - centre)).astype(BF16)
                sums.append((cols, v, q, d, probability.astype(BF16), dscores))
            for cols, v, q, d, rounded, dscores in sums:
                out = dot_tn(rounded, v)
                att_ref[mine, cols] = jnp.concatenate(
                    [out[:block, :HD], out[block:, HD:]], axis=1
                ).astype(BF16)
                value_grads = dot(rounded, d).astype(BF16)
                key_grads = (dot(dscores, q) * scale).astype(BF16)
                for i, (ref, b) in enumerate(bands(near_dk, far_dk, c)):
                    ref[b, cols] = key_grads[i * part : (i + 1) * part]
                for i, (ref, b) in enumerate(bands(near_dv, far_dv, c)):
                    ref[b, cols] = value_grads[i * part : (i + 1) * part]
        return carry

    lax.fori_loop(0, count, stretch, 0)


def attend(near, far, w_key, w_value, tokens, first, count):
    width, feats = w_key.shape
    rows = near[0].shape[0]
    return pl.pallas_call(
        functools.partial(attend_kernel, len(far), first, count, len(tokens) - 2),
        in_specs=[vmem()] * (4 + len(far) + len(tokens)),
        out_specs=[vmem()] * 5,
        out_shape=[jax.ShapeDtypeStruct((count * STRETCH, feats), BF16)]
        + [jax.ShapeDtypeStruct((rows, feats), BF16)] * 4,
        scratch_shapes=[pltpu.VMEM((rows, feats), BF16)] * 2
        + [pltpu.VMEM((count * STRETCH, feats), BF16)] * 2,
        compiler_params=params(20),
        cost_estimate=pl.CostEstimate(
            flops=4 * rows * width * feats + 40 * rows * STRETCH * feats,
            bytes_accessed=4 * width * feats + 12 * rows * feats,
            transcendentals=2 * rows * STRETCH * feats // HD,
        ),
        name="attend",
    )(*near, *far, w_key, w_value, *tokens)


def terms_kernel(numbers, *refs):
    count = len(numbers)
    grad_refs, (wk_ref, wv_ref), term_refs = refs[: 2 * count], refs[2 * count : -count], refs[-count:]
    rows = term_refs[0].shape[0]

    def rows_of(refs):
        parts = [ref[pl.ds(number * rows, rows), :] for number, ref in zip(numbers, refs)]
        return jnp.concatenate(parts, axis=0)

    term = dot(rows_of(grad_refs[:count]), wk_ref[...])
    term = term + dot(rows_of(grad_refs[count:]), wv_ref[...])
    term = term.astype(BF16)
    for i, ref in enumerate(term_refs):
        ref[...] = term[i * rows : (i + 1) * rows]


def slot_terms(asked, turned, rows):
    feats, width = turned[0].shape
    count = len(asked)
    return pl.pallas_call(
        functools.partial(terms_kernel, [number for _, _, number in asked]),
        in_specs=[vmem()] * (2 * count + 2),
        out_specs=[vmem()] * count,
        out_shape=[jax.ShapeDtypeStruct((rows, width), BF16)] * count,
        compiler_params=params(20),
        cost_estimate=pl.CostEstimate(
            flops=4 * count * rows * width * feats,
            bytes_accessed=4 * width * feats + 2 * count * rows * (width + 2 * feats),
            transcendentals=0,
        ),
        name="slot_terms",
    )(*[keys for keys, _, _ in asked], *[values for _, values, _ in asked], *turned)


def stage_kernel(
    gain_ref, x_ref, w_in_ref, w_out_ref, inv_ref, slope_ref, w_in_turned, w_out_turned, normed
):
    rows, width = x_ref.shape
    normed[...], inv_ref[...] = norm_of(
        x_ref[...].astype(F32), gain_ref[...].reshape(1, width)
    )
    for at, part in tiles(w_in_ref.shape[1], 256):
        cols = pl.ds(at, part)
        pre = dot(normed[...], w_in_ref[:, cols])
        square = pre * pre
        tanh = jnp.tanh(GELU_A * pre * (1.0 + GELU_B * square))
        slope_ref[:, cols] = 0.5 * (1.0 + tanh) + 0.5 * pre * (1.0 - tanh * tanh) * (
            GELU_A * (1.0 + 3.0 * GELU_B * square)
        )
        w_in_turned[cols, :] = w_in_ref[:, cols].T
        w_out_turned[:, cols] = w_out_ref[cols, :].T


def stage(flat_rows, enc_gain, w_in, w_out):
    rows, width = flat_rows.shape
    hidden = w_in.shape[1]
    return pl.pallas_call(
        stage_kernel,
        in_specs=[vmem()] * 4,
        out_specs=[vmem()] * 4,
        out_shape=[
            jax.ShapeDtypeStruct((rows, 1), F32),
            jax.ShapeDtypeStruct((rows, hidden), F32),
            jax.ShapeDtypeStruct((hidden, width), BF16),
            jax.ShapeDtypeStruct((width, hidden), BF16),
        ],
        scratch_shapes=[pltpu.VMEM((rows, width), BF16)],
        compiler_params=params(24),
        cost_estimate=pl.CostEstimate(
            flops=2 * rows * width * hidden,
            bytes_accessed=8 * width * hidden + 4 * rows * hidden + 4 * rows * width,
            transcendentals=rows * hidden,
        ),
        name="stage",
    )(enc_gain, flat_rows, w_in, w_out)


def encode_back_kernel(
    masks, ids_ref, me_ref, gain_ref, x_ref, inv_ref, slope_ref, w_in_turned, w_out_turned, *refs
):
    arrived_refs, (out_ref, row_grad, upstream, d_pre) = refs[:-4], refs[-4:]
    capacity, piece, width = arrived_refs[0].shape
    row_count = row_grad.shape[0]
    rows = x_ref.shape[0]
    row_grad[...] = jnp.zeros_like(row_grad)
    me = me_ref[0]
    for mask, ref in zip(masks, arrived_refs):

        def add(row, place):
            row_grad[row] += ref[place].astype(F32)

        each_request(ids_ref, me ^ mask, me * row_count, row_count, capacity, add)
    upstream[...] = row_grad[...].reshape(upstream.shape).astype(BF16)
    d_act = []
    bands = [pl.ds(at, part) for at, part in tiles(w_out_turned.shape[1], 256)]
    for i in range(len(bands) + 1):
        if i < len(bands):
            d_act.append(dot(upstream[...], w_out_turned[:, bands[i]]))
        if i > 0:
            cols = bands[i - 1]
            d_pre[:, cols] = (d_act[i - 1] * slope_ref[:, cols]).astype(BF16)
    gain = gain_ref[...].reshape(1, width)
    d_norm = []
    bands = tiles(rows, 128)
    for i in range(len(bands) + 1):
        if i < len(bands):
            d_norm.append(dot(d_pre[pl.ds(*bands[i]), :], w_in_turned[...]))
        if i > 0:
            at, part = bands[i - 1]
            band = pl.ds(at, part)
            scaled = d_norm[i - 1] * gain
            x = x_ref[band, :].astype(F32)
            inverse = inv_ref[band, :]
            mean = jnp.mean(scaled * x, axis=-1, keepdims=True)
            back = inverse * scaled - x * (inverse * inverse * inverse * mean)
            summed = row_grad[at // piece : (at + part) // piece].reshape(part, width)
            out_ref[band, :] = (summed + back).astype(BF16)


def encode_back(all_ids, me, enc_gain, flat_rows, staged, arrived, masks):
    rows, hidden = staged[1].shape
    _, piece, width = arrived[0].shape
    return pl.pallas_call(
        functools.partial(encode_back_kernel, masks),
        in_specs=[smem(), smem()] + [vmem()] * (6 + len(arrived)),
        out_specs=vmem(),
        out_shape=jax.ShapeDtypeStruct((rows, width), BF16),
        scratch_shapes=[
            pltpu.VMEM((rows // piece, piece, width), F32),
            pltpu.VMEM((rows, width), BF16),
            pltpu.VMEM((rows, hidden), BF16),
        ],
        compiler_params=params(28),
        cost_estimate=pl.CostEstimate(
            flops=4 * rows * width * hidden,
            bytes_accessed=4 * width * hidden + 4 * rows * hidden + 8 * rows * width,
            transcendentals=0,
        ),
        name="encode_back",
    )(all_ids, me, enc_gain, flat_rows, *staged, *arrived)


def shift(value, axis, by):
    peers = lax.axis_size(axis)
    pairs = [(i, i + by) for i in range(peers) if 0 <= i + by < peers]
    return lax.ppermute(value, axis, pairs)


def swap(value, axis, bit):
    return lax.ppermute(value, axis, [(i, i ^ bit) for i in range(lax.axis_size(axis))])


def exchange(buffers, masks, later, between=None):
    axes = ("role", "seq")
    count = len(buffers)
    arrived = [buffers[0]] + [swap(buffers[k], axes, masks[k]) for k in range(1, count - 2)]
    for early, k in ((1, count - 2), (2, count - 1)):
        arrived[early], value, later = lax.optimization_barrier((arrived[early], buffers[k], later))
        arrived.append(swap(value, axes, masks[k]))
        if early == 1 and between is not None:
            later = between(later)
    return arrived, later


def add_up(shares):
    if len(shares) == 1:
        return shares[0]
    return functools.reduce(jnp.add, [share.astype(F32) for share in shares]).astype(BF16)


def body(hidden, w_query, w_key, w_value, enc_gain, w_in, w_out, db_states, neighbours, d_attended):
    groups = lax.axis_size(("role", "seq"))
    shards = lax.axis_size("tp")
    me = lax.axis_index(("role", "seq")).astype(jnp.int32).reshape(1)
    masks = exchange_masks(groups, lax.axis_size("seq"))
    row_count, piece, width = db_states.shape
    stretch_count, fan_out = neighbours.shape
    slots = stretch_count * fan_out
    tokens = hidden.shape[0]
    edge = STRETCH - 1
    capacity = max(2, 2 * ((stretch_count - 1 + groups - 2) // (groups - 1)))
    neighbours = neighbours.T
    all_ids = lax.all_to_all(
        jnp.broadcast_to(neighbours[None], (groups, fan_out, stretch_count)),
        ("role", "seq"), 0, 0, tiled=True,
    )
    flat_rows = db_states.reshape(row_count * piece, width)
    encoded = encode(flat_rows, enc_gain, w_in, w_out)
    *outgoing, hidden = send_rows(
        all_ids, me, encoded.reshape(row_count, piece, width), hidden, capacity, masks
    )
    arrived, (partial, hidden) = exchange(
        outgoing, masks, hidden, lambda tokens: (query_first(tokens, w_query), tokens)
    )
    queries, edges = query_last(hidden, partial, w_query, d_attended)
    queries, neighbours = lax.optimization_barrier((queries, neighbours))
    count = stretch_count // 2
    first_own, last_own = [
        value.reshape(slots * piece // 2, width)
        for value in pick_rows(neighbours, me, arrived, row_count, masks, 2)
    ]
    first_own, edges = lax.optimization_barrier((first_own, edges))
    edges = shift(edges, "seq", -1)
    bits = [1 << i for i in range(shards.bit_length() - 1)]
    half = shards // 2

    def gathered(pieces):
        for bit in reversed(bits[:-1]):
            pieces.update({mask | bit: swap(pieces[mask], "tp", bit) for mask in list(pieces)})
        return [pieces[mask] for mask in sorted(pieces)]

    first_far = swap(first_own, "tp", half)
    first_near = gathered({0: first_own})
    last_far = swap(last_own, "tp", half)
    last_near = gathered({0: last_own})
    (first_kv, last_kv), turned = project([first_near, last_near], w_key, w_value)
    first_far, first_kv, last_kv = lax.optimization_barrier((first_far, first_kv, last_kv))
    first_far = gathered({half: first_far})
    first_far[-1], edges = lax.optimization_barrier((first_far[-1], edges))
    first_o, *first_grads = attend(
        first_kv, first_far, w_key, w_value, (queries, d_attended), 0, count
    )
    first_o, last_far = lax.optimization_barrier((first_o, last_far))
    last_far = gathered({half: last_far})

    rows = slots * piece // 2

    def fold(shares):
        for bit in bits[:-1]:
            for mask in sorted([mask for mask in shares if mask & bit], reverse=True):
                shares[mask ^ bit].append(swap(add_up(shares.pop(mask)), "tp", bit))
        return shares[0]

    def to_send(grads, others, tied):
        numbers = list(reversed(range(1, half)))
        asked = [(grads[2], grads[3], j) for j in numbers]
        asked += [(each[0], each[1], j) for each in others for j in numbers]
        terms = slot_terms(asked, turned, rows)
        sums = []
        for i in range(1 + len(others)):
            mine = terms[i * len(numbers) : (i + 1) * len(numbers)]
            sums.append({0: [], **{j: [term] for j, term in zip(numbers, mine)}})
        tied, grads = lax.optimization_barrier((tied, grads))
        sums[0][0] = list(slot_terms([(grads[2], grads[3], 0)], turned, rows))
        far, *near = [fold(shares) for shares in sums]
        return add_up(far), near, tied

    sent, _, edges = to_send(first_grads, [], edges)
    sent, edges = lax.optimization_barrier((sent, edges))
    first_back = swap(sent, "tp", half)
    last_o, *last_grads = attend(
        last_kv, last_far, w_key, w_value, (queries, d_attended, edges), count, count
    )
    o_edge = shift(last_o[last_o.shape[0] - STRETCH :], "seq", 1)
    sent, near_back, first_back = to_send(last_grads, [first_grads, last_grads], first_back)
    last_back = swap(sent, "tp", half)
    own_terms = slot_terms(
        [(grads[0], grads[1], 0) for grads in (first_grads, last_grads)], turned, rows
    )
    shares = [list(own_terms)] + [list(pair) for pair in zip(*near_back)]
    shares.append([first_back, last_back])
    shares = [[part.reshape(-1, piece, width) for part in share] for share in shares]
    outgoing_grads = return_grads(neighbours, me, shares, row_count, masks, capacity)
    attended = jnp.concatenate([o_edge[1:], first_o, last_o[: last_o.shape[0] - edge]], axis=0)
    totals, flat_rows = exchange(outgoing_grads, masks, flat_rows)
    staged = stage(flat_rows, enc_gain, w_in, w_out)
    grads = encode_back(all_ids, me, enc_gain, flat_rows, staged, totals, masks)
    return (attended, grads.reshape(row_count, piece, width))


def solution(mesh):
    in_specs = (
        P(("role", "seq"), None),
        P(None, "tp"),
        P(None, "tp"),
        P(None, "tp"),
        P(),
        P(),
        P(),
        P(("role", "seq"), "tp", None),
        P(("role", "seq"), None),
        P(("role", "seq"), "tp"),
    )
    out_specs = (P(("role", "seq"), "tp"), P(("role", "seq"), "tp", None))
    return jax.shard_map(body, mesh=mesh, in_specs=in_specs, out_specs=out_specs, check_vma=False)
```
